512 devices in a mesh: section: 16 (over z), seq: 32 (over x, y, core).
Axes of the slice: x: 4, y: 4, z: 16, core: 2. Of those that a mesh axis runs over, the one named last changes fastest.
Arguments:
- pre_act: bfloat16 [16, 8192, 4096], P('section', 'seq'), may hold values from -6 to 6
- out_grad: bfloat16 [16, 8192, 1024], P('section', 'seq'), may hold values from -6 to 6
- proj_weight: bfloat16 [16, 1024, 4096], P('section', 'seq'), may hold values from -0.1875 to 0.1875
- lengths: int32 [16, 32], P('section'), may hold values from 0 to 512, as said below
- link_bits: int32 [16, 32], P('section', 'seq'), may hold values 0 or 1
Outputs:
- passed: bfloat16 [16, 8192, 1024], P('section', 'seq')
The draws below stay inside these ranges and needn't reach their ends.
Inputs may be any that keep to these rules, and one draw needn't show every extreme that they name: `lengths`: one row a section: positive entries come first, then zeros; the users they describe fill the section's 32 tiles exactly, each taking ceil(length / 256) consecutive tiles, so no history spans more than 2 tiles; the first user of every section has 512 actions.
All inputs are finite; a program needn't handle non-finite values. No bound on the sum of `link_bits` on one device may be relied on, other than what follows from the above.
Results may differ from the reference program's by a relative error of at most 0.01.
Values may be sent and summed in bfloat16 or wider, within the bound.
A program may use at most 128 MiB of HBM per device.

```python
import jax
import jax.numpy as jnp
from jax import lax

D = 1024
HEADS = 8
HEAD_DIM = 128
TILE = 256
MAXT = 2
SECTIONS = 16
NT_TOTAL = 32
TOKENS = 8192


def draw_lengths(key, part):
    key = jax.random.fold_in(key, 11)
    section_keys = jax.random.split(key, SECTIONS)

    def one_section(section_key):
        count_key, tail_key = jax.random.split(section_key)
        slots = jnp.arange(NT_TOTAL, dtype=jnp.int32)
        spans = jax.random.randint(count_key, (NT_TOTAL,), 1, MAXT + 1, dtype=jnp.int32)
        spans = jnp.where(slots == 0, MAXT, spans).astype(jnp.int32)
        span_ends = jnp.cumsum(spans).astype(jnp.int32)
        starts = span_ends - spans
        live = starts < NT_TOTAL
        kept = jnp.where(live, jnp.minimum(spans, NT_TOTAL - starts), 0).astype(jnp.int32)
        tails = jax.random.randint(tail_key, (NT_TOTAL,), 1, TILE + 1, dtype=jnp.int32)
        tails = jnp.where(slots == 0, TILE, tails).astype(jnp.int32)
        return jnp.where(live, (kept - 1) * TILE + tails, 0).astype(jnp.int32)
    return jax.vmap(one_section)(section_keys)


def touch_ends(result, stream_key, least, high):
    shape = result.shape
    spot = [jax.random.randint(jax.random.fold_in(stream_key, axis), (), 0, shape[axis]) for axis in range(len(shape))]
    result = result.at[tuple(spot)].set(least)
    longest = shape.index(max(shape))
    spot[longest] = (spot[longest] + 1) % shape[longest]
    return result.at[tuple(spot)].set(high)


def block_scale(rng, dims, cuts, least, top_value):
    loudness, own = 1.0, jax.random.fold_in(rng, 6)
    for position, shards_of in cuts:
        draws = jnp.exp(jax.random.uniform(jax.random.fold_in(own, position), (shards_of,), jnp.float32, least / len(cuts), top_value / len(cuts)))
        loudness = loudness * jnp.repeat(draws, dims[position] // shards_of).reshape([-1 if axis == position else 1 for axis in range(len(dims))])
    return loudness


def bell_draw(own_key, shape, spread, bound, cuts=(), kind=jnp.bfloat16):
    values = jax.random.normal(own_key, shape, jnp.float32) * spread
    if len(cuts) > 0:
        values = block_scale(own_key, shape, cuts, -0.22, 0.18) * values
    return jnp.clip(values, min=-bound, max=bound).astype(kind)


def setup_inputs(seed: int = 0) -> dict:
    splits = jax.random.split(jax.random.key(seed), 6)
    pre_act = bell_draw(splits[0], (SECTIONS, TOKENS, 4 * D), 1.0, 6.0, ((0, 16), (1, 32)))
    out_grad = bell_draw(splits[1], (SECTIONS, TOKENS, D), 1.0, 6.0, ((0, 16), (1, 32)))
    proj_weight = bell_draw(splits[2], (SECTIONS, D, 4 * D), D ** -0.5, 0.1875, ((0, 16), (1, 32)))
    lengths = draw_lengths(jax.random.fold_in(splits[5], 71), 0)
    link_bits = touch_ends((jax.random.randint(splits[4], (SECTIONS, NT_TOTAL), 0, 4) < 3).astype(jnp.int32), jax.random.fold_in(splits[4], 1), 0, 1)
    return dict(pre_act=pre_act, out_grad=out_grad, proj_weight=proj_weight, lengths=lengths, link_bits=link_bits)


EPSILON = 1e-05

def silu_slope(values):
    sigmoid_val = jax.nn.sigmoid(values)
    return sigmoid_val * (1.0 + values * (1.0 - sigmoid_val))

def tile_facts(lengths, first_tile, tile_count):
    tile_ids = first_tile + jnp.arange(tile_count, dtype=jnp.int32)
    tile_spans = ((lengths + (TILE - 1)) // TILE).astype(jnp.int32)
    span_ends = jnp.cumsum(tile_spans).astype(jnp.int32)
    owner_user = lax.optimization_barrier(jnp.sum((span_ends[None, :] <= tile_ids[:, None]).astype(jnp.int32), axis=1))
    user_pick = (jnp.arange(lengths.shape[0], dtype=jnp.int32)[None, :] == owner_user[:, None]).astype(jnp.int32)
    starts = lax.optimization_barrier(jnp.sum(user_pick * (span_ends - tile_spans)[None, :], axis=1))
    totals = lax.optimization_barrier(jnp.sum(user_pick * lengths[None, :], axis=1))
    tile_place = tile_ids - starts
    valid_rows = jnp.minimum(totals - tile_place * TILE, TILE)
    return (tile_place, valid_rows)

def tile_masks(tile_place, valid_rows, link_bits):
    row_ids = jnp.arange(TILE, dtype=jnp.int32)
    row_ok = row_ids[None, :] < valid_rows[:, None]
    causal = row_ids[:, None] >= row_ids[None, :]
    same_mask = row_ok[:, :, None] & row_ok[:, None, :] & causal[None]
    linked = (tile_place >= 1) & (link_bits == 1)
    cross_mask = linked[:, None, None] & row_ok[:, :, None] & jnp.ones((1, 1, TILE), dtype=bool)
    return (row_ok.astype(jnp.float32), same_mask.astype(jnp.float32), cross_mask.astype(jnp.float32))

def attend_forward(queries, keys_in, values_in, mask, score_scale):
    scores = jnp.einsum('tihd,tjhd->thij', queries.astype(jnp.float32), keys_in.astype(jnp.float32)) * score_scale
    weights = (jax.nn.silu(scores) * mask[:, None] / TILE).astype(jnp.bfloat16)
    mixed = jnp.einsum('thij,tjhd->tihd', weights.astype(jnp.float32), values_in.astype(jnp.float32))
    return (scores, weights, mixed)

def attend_backward(grad_mix, queries, keys_in, values_in, scores, weights, mask, score_scale):
    grad_mix_f = grad_mix.astype(jnp.float32)
    grad_val = jnp.einsum('thij,tihd->tjhd', weights.astype(jnp.float32), grad_mix_f).astype(jnp.bfloat16)
    grad_att = jnp.einsum('tihd,tjhd->thij', grad_mix_f, values_in.astype(jnp.float32))
    grad_score = (grad_att * mask[:, None] / TILE * silu_slope(scores)).astype(jnp.bfloat16)
    grad_score_f = grad_score.astype(jnp.float32)
    grad_query = jnp.einsum('thij,tjhd->tihd', grad_score_f, keys_in.astype(jnp.float32)) * score_scale
    grad_key = (jnp.einsum('thij,tihd->tjhd', grad_score_f, queries.astype(jnp.float32)) * score_scale).astype(jnp.bfloat16)
    return (grad_query, grad_val, grad_key)

def one_section(pre_act, out_grad, proj_weight, lengths, link_bits):
    tile_count = pre_act.shape[0] // TILE
    tile_place, valid_rows = tile_facts(lengths, 0, tile_count)
    row_ok, same_mask, cross_mask = tile_masks(tile_place, valid_rows, link_bits)
    pre_tiles = pre_act.reshape(tile_count, TILE, 4 * D).astype(jnp.float32)
    activated = jax.nn.silu(pre_tiles).astype(jnp.bfloat16)
    gate_u = activated[:, :, :D]
    values_in = activated[:, :, D:2 * D].reshape(tile_count, TILE, HEADS, HEAD_DIM)
    queries = activated[:, :, 2 * D:3 * D].reshape(tile_count, TILE, HEADS, HEAD_DIM)
    keys_in = activated[:, :, 3 * D:].reshape(tile_count, TILE, HEADS, HEAD_DIM)
    key_prev = jnp.concatenate([jnp.zeros_like(keys_in[:1]), keys_in[:-1]], axis=0)
    val_prev = jnp.concatenate([jnp.zeros_like(values_in[:1]), values_in[:-1]], axis=0)
    score_scale = HEAD_DIM ** (-0.5)
    same_scores, same_weights, same_mixed = attend_forward(queries, keys_in, values_in, same_mask, score_scale)
    cross_scores, cross_weights, cross_mixed = attend_forward(queries, key_prev, val_prev, cross_mask, score_scale)
    mixed = (same_mixed + cross_mixed).reshape(tile_count, TILE, D)
    row_mean = lax.optimization_barrier(jnp.mean(mixed, axis=-1, keepdims=True))
    centered = mixed - row_mean
    inv_std = lax.rsqrt(lax.optimization_barrier(jnp.mean(centered * centered, axis=-1, keepdims=True)) + EPSILON)
    normed = centered * inv_std
    cotangent = out_grad.reshape(tile_count, TILE, D).astype(jnp.float32) * row_ok[:, :, None]
    grad_gate = cotangent * normed
    grad_norm = cotangent * gate_u.astype(jnp.float32)
    grad_mix = inv_std * (grad_norm - lax.optimization_barrier(jnp.mean(grad_norm, axis=-1, keepdims=True)) - normed * lax.optimization_barrier(jnp.mean(grad_norm * normed, axis=-1, keepdims=True)))
    grad_mix = grad_mix.astype(jnp.bfloat16).reshape(tile_count, TILE, HEADS, HEAD_DIM)
    query_same, val_same, key_same = attend_backward(grad_mix, queries, keys_in, values_in, same_scores, same_weights, same_mask, score_scale)
    query_cross, val_cross, key_cross = attend_backward(grad_mix, queries, key_prev, val_prev, cross_scores, cross_weights, cross_mask, score_scale)
    val_next = jnp.concatenate([val_cross[1:], jnp.zeros_like(val_cross[:1])], axis=0)
    key_next = jnp.concatenate([key_cross[1:], jnp.zeros_like(key_cross[:1])], axis=0)
    grad_value = val_same.astype(jnp.float32) + val_next.astype(jnp.float32)
    grad_key = key_same.astype(jnp.float32) + key_next.astype(jnp.float32)
    grad_query = query_same + query_cross
    shape_rows = (tile_count, TILE, D)
    grads = jnp.concatenate([grad_gate, grad_value.reshape(shape_rows), grad_query.reshape(shape_rows), grad_key.reshape(shape_rows)], axis=-1) * silu_slope(pre_tiles)
    grads = grads.astype(jnp.bfloat16).reshape(tile_count * TILE, 4 * D)
    grad_in = lax.dot_general(grads, proj_weight, (((1,), (1,)), ((), ())), preferred_element_type=jnp.float32)
    return grad_in.astype(jnp.bfloat16)

def reference(pre_act, out_grad, proj_weight, lengths, link_bits):
    local_grads = lax.map(lambda operands: one_section(*operands), (pre_act, out_grad, proj_weight, lengths, link_bits))
    return jnp.concatenate([local_grads[1:], jnp.zeros_like(local_grads[:1])], axis=0)
```

```python
import jax
import jax.numpy as jnp
from jax import lax
from jax.experimental import pallas as pl
from jax.experimental.pallas import tpu as pltpu
from jax.sharding import PartitionSpec as P

D = 1024
HEADS = 8
HEAD_DIM = 128
TILE = 256
SIDE = 4
SECTIONS = 16
DEVICES = 32
SHARD = D // DEVICES
EPSILON = 1e-05
MESH = pl.DeviceIdType.MESH
F32 = jnp.float32
BF16 = jnp.bfloat16
SCALE = HEAD_DIM ** (-0.5)

PIECE = 256
PIECES = D // PIECE

A_FROM = {-1: 0, 1: 1}
A_FAR = (2, 3)
LANES = (0, -1, 1, 2)
B_FROM = {(a, s): 4 + 4 * i + j for i, a in enumerate(LANES) for j, s in enumerate((-1, 1))}
B_FAR = {(a, h): 4 + 4 * i + 2 + h for i, a in enumerate(LANES) for h in range(2)}
SWAP = {(a, b): 20 + 4 * i + j for i, a in enumerate(LANES) for j, b in enumerate(LANES)}
K_IN = 36
V_IN = 40
Q_IN = 44
DO_IN = 48
OUT = 52
TRANSFERS = 56


def mod(value, size):
    return lax.rem(value + size, size)


def dot_nn(a, b):
    return lax.dot_general(a, b, (((1,), (0,)), ((), ())), preferred_element_type=F32)


def dot_nt(a, b):
    return lax.dot_general(a, b, (((1,), (1,)), ((), ())), preferred_element_type=F32)


def dot_tn(a, b):
    return lax.dot_general(a, b, (((0,), (0,)), ((), ())), preferred_element_type=F32)


def sigmoid(values):
    return 0.5 * jnp.tanh(0.5 * values) + 0.5


def kernel(
    len_ref, link_ref, pre, og, w, out,
    pre_v, og_v, wbuf, kraw, vraw, qraw, doraw, kbuf, vbuf, qbuf, dobuf, gate_buf, slopes,
    p_same, s_same, p_cross, s_cross, mix, grads, staged,
    send_sem, recv_sem, local_sem,
):
    section = lax.axis_index("section")
    me = lax.axis_index("seq")
    core = lax.rem(me, 2)
    cy = lax.rem(lax.div(me, 2), SIDE)
    cx = lax.div(me, 2 * SIDE)
    other = me + 1 - 2 * core
    after = mod(me + 1, DEVICES)
    before = mod(me - 1, DEVICES)

    def at(a, b, c=None):
        c = core if c is None else c
        x = mod(cx + a * (1 - c) + b * c, SIDE)
        y = mod(cy + a * c + b * (1 - c), SIDE)
        return (x * SIDE + y) * 2 + c

    def rows(device, half=None):
        if half is None:
            return pl.ds(pl.multiple_of(device * SHARD, SHARD), SHARD)
        size = SHARD // 2
        return pl.ds(pl.multiple_of(device * SHARD + half * size, size), size)

    barrier = pltpu.get_barrier_semaphore()
    peers = [
        {"seq": other},
        {"seq": at(1, 0)},
        {"seq": at(-1, 0)},
        {"seq": at(0, 1)},
        {"seq": at(0, -1)},
        {"seq": after + (before - after) * (1 - core)},
        {"section": mod(section + 1, SECTIONS)},
        {"section": mod(section - 1, SECTIONS)},
    ]

    local = [
        pltpu.make_async_copy(pre.at[0, :, pl.ds(D * i, D)], pre_v.at[:, pl.ds(D * i, D)], local_sem.at[i])
        for i in range(4)
    ]
    local.append(pltpu.make_async_copy(og.at[0], og_v, local_sem.at[4]))
    local.append(pltpu.make_async_copy(w.at[0], wbuf.at[rows(me)], local_sem.at[5]))
    for i in (3, 1, 2, 0, 4, 5):
        local[i].start()
    for peer in peers:
        pl.semaphore_signal(barrier, inc=1, device_id=peer, device_id_type=MESH)
    pl.semaphore_wait(barrier, len(peers))

    sent = []

    def copy(src, dst, number, target):
        return pltpu.make_async_remote_copy(
            src_ref=src, dst_ref=dst, send_sem=send_sem.at[number], recv_sem=recv_sem.at[number],
            device_id=target, device_id_type=MESH,
        )

    def send(src, dst, number, target):
        moved = copy(src, dst, number, {"seq": target})
        moved.start()
        sent.append(moved)

    def arrived(dst, number):
        copy(dst, dst, number, {"seq": other}).wait_recv()

    def columns(i):
        return pl.ds(PIECE * i, PIECE)

    for i in range(PIECES):
        send(pre.at[0, :, pl.ds(3 * D + PIECE * i, PIECE)], kraw.at[:, columns(i)], K_IN + i, after)
        send(pre.at[0, :, pl.ds(D + PIECE * i, PIECE)], vraw.at[:, columns(i)], V_IN + i, after)
        send(pre.at[0, :, pl.ds(2 * D + PIECE * i, PIECE)], qraw.at[:, columns(i)], Q_IN + i, before)

    def block(device, half=None):
        return wbuf.at[rows(device, half)]

    def pass_on(src, a, b):
        send(src, block(at(a, b)), SWAP[a, b], other)

    def spread(src, a):
        send(src, block(at(a, 0)), B_FROM[a, -1], at(0, 1))
        send(src, block(at(a, 0)), B_FROM[a, 1], at(0, -1))
        pass_on(src, a, 0)

    def own_out():
        send(w.at[0], block(me), A_FROM[-1], at(1, 0))
        send(w.at[0], block(me), A_FROM[1], at(-1, 0))
        spread(w.at[0], 0)

    def first_axis():
        arrived(block(at(-1, 0)), A_FROM[-1])
        send(block(at(-1, 0), 0), block(at(-1, 0), 0), A_FAR[0], at(1, 0))
        arrived(block(at(1, 0)), A_FROM[1])
        send(block(at(1, 0), 1), block(at(1, 0), 1), A_FAR[1], at(-1, 0))
        spread(block(at(-1, 0)), -1)
        spread(block(at(1, 0)), 1)

    def first_axis_far():
        for half in range(2):
            arrived(block(at(2, 0), half), A_FAR[half])
        spread(block(at(2, 0)), 2)

    def second_axis(a):
        for half, step in enumerate((-1, 1)):
            arrived(block(at(a, step)), B_FROM[a, step])
            send(block(at(a, step), half), block(at(a, step), half), B_FAR[a, half], at(0, -step))
            pass_on(block(at(a, step)), a, step)

    def second_axis_far(a):
        for half in range(2):
            arrived(block(at(a, 2), half), B_FAR[a, half])
        pass_on(block(at(a, 2)), a, 2)

    def swapped(a, b):
        arrived(block(at(a, b, 1 - core)), SWAP[a, b])

    own_out()

    end = jnp.int32(0)
    place = jnp.int32(0)
    total = jnp.int32(0)
    for user in range(DEVICES):
        length = len_ref[0, user]
        begin = end
        end = begin + lax.div(length + (TILE - 1), TILE)
        mine = jnp.logical_and(begin <= me, me < end)
        place = jnp.where(mine, me - begin, place)
        total = jnp.where(mine, length, total)
    valid = jnp.minimum(total - place * TILE, TILE)
    linked = jnp.where(jnp.logical_and(place >= 1, link_ref[0, 0] == 1), 1, 0).astype(jnp.int32)
    takes = linked.astype(F32)
    gives = 1.0 - takes

    def activate(group, target):
        def step(i, carry):
            at_rows = pl.ds(pl.multiple_of(i * 32, 32), 32)
            value = pre_v[at_rows, pl.ds(D * group, D)].astype(F32)
            s = sigmoid(value)
            act = value * s
            target[at_rows, :] = act.astype(BF16)
            slopes[at_rows, pl.ds(D * group, D)] = s + act * (1.0 - s)
            return carry
        lax.fori_loop(0, TILE // 32, step, 0)

    for group, target in ((3, kbuf.at[0]), (1, vbuf.at[0]), (2, qbuf.at[0]), (0, gate_buf)):
        local[group].wait()
        activate(group, target)
    local[4].wait()
    local[5].wait()

    def head_columns(h):
        return pl.ds(pl.multiple_of(h * HEAD_DIM, HEAD_DIM), HEAD_DIM)

    row_ids = lax.broadcasted_iota(jnp.int32, (TILE, TILE), 0)
    col_ids = lax.broadcasted_iota(jnp.int32, (TILE, TILE), 1)

    def weigh(scores, causal):
        z = scores * SCALE
        s = sigmoid(z)
        p = z * s
        slope = s + p * (1.0 - s)
        if causal:
            keep = col_ids <= row_ids
            p = jnp.where(keep, p, 0.0)
            slope = jnp.where(keep, slope, 0.0)
        return p.astype(BF16), slope.astype(BF16)

    def same_forward(h, carry):
        cols = head_columns(h)
        p, slope = weigh(dot_nt(qbuf[0, :, cols], kbuf[0, :, cols]), True)
        p_same[h] = p
        s_same[h] = slope
        mix[:, cols] = dot_nn(p, vbuf[0, :, cols]) * (1.0 / TILE)
        return carry

    def cross_forward(h, carry):
        cols = head_columns(h)
        p, slope = weigh(dot_nt(qbuf[1 - linked, :, cols], kbuf[linked, :, cols]), False)
        p_cross[h] = p
        s_cross[h] = slope
        mix[:, cols] += dot_nn(p, vbuf[linked, :, cols]) * (takes / TILE)
        return carry

    def same_backward(h, carry):
        cols = head_columns(h)
        do = dobuf[0, :, cols]
        ds = (dot_nt(do, vbuf[0, :, cols]) * s_same[h].astype(F32)).astype(BF16)
        s_same[h] = ds
        return carry

    def finish(h, carry):
        cols = head_columns(h)
        do = dobuf[0, :, cols]
        dox = dobuf[1 - linked, :, cols]
        qx, kx, vx = qbuf[1 - linked, :, cols], kbuf[linked, :, cols], vbuf[linked, :, cols]
        ds = s_same[h]
        dsx = (dot_nt(dox, vx) * s_cross[h].astype(F32)).astype(BF16)
        dv = (dot_tn(p_same[h], do) + dot_tn(p_cross[h], dox) * gives) * (1.0 / TILE)
        dk = (dot_tn(ds, qbuf[0, :, cols]) + dot_tn(dsx, qx) * gives) * (SCALE / TILE)
        dq = (dot_nn(ds, kbuf[0, :, cols]) + dot_nn(dsx, kx) * takes) * (SCALE / TILE)
        for i, value in ((1, dv), (2, dq), (3, dk)):
            there = pl.ds(pl.multiple_of(D * i + h * HEAD_DIM, HEAD_DIM), HEAD_DIM)
            grads[:, there] = (value * slopes[:, there]).astype(BF16)
        return carry

    first_axis()
    lax.fori_loop(0, 4, same_forward, 0)
    second_axis(0)
    lax.fori_loop(4, 8, same_forward, 0)
    first_axis_far()
    second_axis(-1)

    for i in range(PIECES):
        for raw, target, number in ((kraw, kbuf, K_IN), (vraw, vbuf, V_IN), (qraw, qbuf, Q_IN)):
            arrived(raw.at[:, columns(i)], number + i)
            value = raw[:, columns(i)].astype(F32)
            target[1, :, columns(i)] = (value * sigmoid(value)).astype(BF16)
        lax.fori_loop(2 * i, 2 * i + 2, cross_forward, 0)

    def norm(i, carry):
        at_rows = pl.ds(pl.multiple_of(i * 32, 32), 32)
        mixed = mix[at_rows, :]
        centered = mixed - jnp.mean(mixed, axis=-1, keepdims=True)
        inv_std = lax.rsqrt(jnp.mean(centered * centered, axis=-1, keepdims=True) + EPSILON)
        normed = centered * inv_std
        live = lax.broadcasted_iota(jnp.int32, (32, 1), 0) + i * 32 < valid
        cot = jnp.where(live, og_v[at_rows, :].astype(F32), 0.0)
        grads[at_rows, pl.ds(0, D)] = (cot * normed * slopes[at_rows, pl.ds(0, D)]).astype(BF16)
        grad_norm = cot * gate_buf[at_rows, :].astype(F32)
        grad_mix = inv_std * (
            grad_norm
            - jnp.mean(grad_norm, axis=-1, keepdims=True)
            - normed * jnp.mean(grad_norm * normed, axis=-1, keepdims=True)
        )
        dobuf[0, at_rows, :] = grad_mix.astype(BF16)
        kraw[at_rows, :] = (grad_mix * takes).astype(BF16)
        return carry

    lax.fori_loop(0, TILE // 32, norm, 0)
    for i in range(PIECES):
        send(kraw.at[:, columns(i)], doraw.at[:, columns(i)], DO_IN + i, before)
    second_axis(1)
    lax.fori_loop(0, 8, same_backward, 0)
    second_axis(2)
    for i in range(PIECES):
        arrived(doraw.at[:, columns(i)], DO_IN + i)
        dobuf[1, :, columns(i)] = doraw[:, columns(i)]
        lax.fori_loop(2 * i, 2 * i + 2, finish, 0)

    for a in LANES:
        second_axis_far(a)
    for a in LANES:
        for b in LANES:
            swapped(a, b)

    def out_copy(i):
        return copy(staged.at[:, columns(i)], out.at[0, :, columns(i)], OUT + i, {"section": mod(section - 1, SECTIONS)})

    for i in range(PIECES):
        weights = wbuf[pl.ds(PIECE * i, PIECE), :]
        staged[:, columns(i)] = dot_nt(grads[...], weights).astype(BF16)

        @pl.when(section > 0)
        def _():
            out_copy(i).start()

    for moved in sent:
        moved.wait_send()

    @pl.when(section > 0)
    def _():
        for i in range(PIECES):
            out_copy(i).wait_send()

    @pl.when(section < SECTIONS - 1)
    def _():
        for i in range(PIECES):
            out_copy(i).wait_recv()

    @pl.when(section == SECTIONS - 1)
    def _():
        mix[...] = jnp.zeros_like(mix)
        kraw[...] = mix[...].astype(BF16)
        zeros = pltpu.make_async_copy(kraw, out.at[0], local_sem.at[0])
        zeros.start()
        zeros.wait()


def body(pre_act, out_grad, proj_weight, lengths, link_bits):
    wide = pltpu.VMEM((TILE, D), BF16)
    pair = pltpu.VMEM((2, TILE, D), BF16)
    scores = pltpu.VMEM((HEADS, TILE, TILE), BF16)
    anywhere = pl.BlockSpec(memory_space=pl.ANY)
    scalars = pl.BlockSpec(memory_space=pltpu.SMEM)
    return pl.pallas_call(
        kernel,
        out_shape=jax.ShapeDtypeStruct((1, TILE, D), BF16),
        in_specs=[scalars, scalars, anywhere, anywhere, anywhere],
        out_specs=anywhere,
        scratch_shapes=[
            pltpu.VMEM((TILE, 4 * D), BF16),
            wide,
            pltpu.VMEM((D, 4 * D), BF16),
            wide, wide, wide, wide,
            pair, pair, pair, pair,
            wide,
            pltpu.VMEM((TILE, 4 * D), F32),
            scores, scores, scores, scores,
            pltpu.VMEM((TILE, D), F32),
            pltpu.VMEM((TILE, 4 * D), BF16),
            wide,
            pltpu.SemaphoreType.DMA((TRANSFERS,)),
            pltpu.SemaphoreType.DMA((TRANSFERS,)),
            pltpu.SemaphoreType.DMA((6,)),
        ],
        compiler_params=pltpu.CompilerParams(
            collective_id=0, has_side_effects=True, vmem_limit_bytes=48 * 1024 * 1024
        ),
    )(lengths, link_bits, pre_act, out_grad, proj_weight)


def solution(mesh):
    placed = (
        P("section", "seq", None),
        P("section", "seq", None),
        P("section", "seq", None),
        P("section", None),
        P("section", "seq"),
    )
    return jax.shard_map(
        body, mesh=mesh, in_specs=placed, out_specs=P("section", "seq", None), check_vma=False
    )
```

```python
import jax
import jax.numpy as jnp
from jax import lax
from jax.experimental import pallas as pl
from jax.experimental.pallas import tpu as pltpu
from jax.sharding import PartitionSpec as P

D = 1024
HEADS = 8
HEAD_DIM = 128
TILE = 256
SIDE = 4
SECTIONS = 16
DEVICES = 32
SHARD = D // DEVICES
EPSILON = 1e-05
MESH = pl.DeviceIdType.MESH
F32 = jnp.float32
BF16 = jnp.bfloat16
SCALE = HEAD_DIM ** (-0.5)

CHUNK = 128
PIECE = 512
GROUP = PIECE // HEAD_DIM
UNROLL = 2

STEPS = (0, -1, 1, 2)
TURN = (-1, 1, -1, 1)

A_IN = 0
B_IN = 3
SWAP = 15
Q_IN = 31
O_IN = 35
DO_IN = 39
DQ_IN = 43
OUT = 47
TRANSFERS = 51


def mod(value, size):
    return lax.rem(value + size, size)


def dot_nn(a, b):
    return lax.dot_general(a, b, (((1,), (0,)), ((), ())), preferred_element_type=F32)


def dot_nt(a, b):
    return lax.dot_general(a, b, (((1,), (1,)), ((), ())), preferred_element_type=F32)


def dot_tn(a, b):
    return lax.dot_general(a, b, (((0,), (0,)), ((), ())), preferred_element_type=F32)


def sigmoid(values):
    return 0.5 * jnp.tanh(0.5 * values) + 0.5


def kernel(
    lengths, link_bits, pre, og, w, out,
    len_ref, link_ref, pre_v, og_v, wbuf, kbuf, vbuf, qbuf, gate_buf, slopes,
    qraw, oraw, doraw, dqraw, qx, dobuf, o_stage, do_stage, dq_stage,
    p_same, s_same, p_cross, s_cross, mix, dq_sum, grads, staged,
    send_sem, recv_sem, local_sem,
):
    section = lax.axis_index("section")
    me = lax.axis_index("seq")
    core = lax.rem(me, 2)
    cy = lax.rem(lax.div(me, 2), SIDE)
    cx = lax.div(me, 2 * SIDE)
    other = me + 1 - 2 * core
    after = mod(me + 1, DEVICES)
    before = mod(me - 1, DEVICES)

    def at(a, b):
        x = mod(cx + a * (1 - core) + b * core, SIDE)
        y = mod(cy + a * core + b * (1 - core), SIDE)
        return (x * SIDE + y) * 2 + core

    def block(device):
        return wbuf.at[pl.ds(pl.multiple_of(device * SHARD, SHARD), SHARD)]

    local = [
        pltpu.make_async_copy(pre.at[0, :, pl.ds(D * i, D)], pre_v.at[:, pl.ds(D * i, D)], local_sem.at[i])
        for i in range(4)
    ]
    local.append(pltpu.make_async_copy(og.at[0], og_v, local_sem.at[4]))
    local.append(pltpu.make_async_copy(w.at[0], block(me), local_sem.at[5]))
    local.append(pltpu.make_async_copy(lengths, len_ref, local_sem.at[6]))
    local.append(pltpu.make_async_copy(link_bits, link_ref, local_sem.at[7]))
    barrier = pltpu.get_barrier_semaphore()
    peers = [
        {"seq": other},
        {"seq": at(1, 0)},
        {"seq": at(-1, 0)},
        {"seq": at(0, 1)},
        {"seq": at(0, -1)},
        {"seq": after + (before - after) * (1 - core)},
        {"section": mod(section + 1, SECTIONS)},
        {"section": mod(section - 1, SECTIONS)},
    ]
    for peer in peers:
        pl.semaphore_signal(barrier, inc=1, device_id=peer, device_id_type=MESH)
    for i in (2, 3, 1, 6, 7, 0, 4, 5):
        local[i].start()
    pl.semaphore_wait(barrier, len(peers))

    sent = []

    def copy(src, dst, number, target):
        return pltpu.make_async_remote_copy(
            src_ref=src, dst_ref=dst, send_sem=send_sem.at[number], recv_sem=recv_sem.at[number],
            device_id=target, device_id_type=MESH,
        )

    def send(src, dst, number, target):
        moved = copy(src, dst, number, {"seq": target})
        moved.start()
        sent.append(moved)

    def arrived(dst, number):
        copy(dst, dst, number, {"seq": other}).wait_recv()

    def chunk(r):
        return pl.ds(CHUNK * r, CHUNK)

    def columns(g):
        return pl.ds(PIECE * g, PIECE)

    def piece(ref, r, g):
        return ref.at[chunk(r), columns(g)]

    def swap(src, i, j):
        send(src, block(at(STEPS[i], STEPS[j])), SWAP + 4 * i + j, other)

    def first_out(src):
        send(src, block(me), A_IN, at(1, 0))

    def first_back(src):
        send(src, block(me), A_IN + 1, at(-1, 0))

    def second_out(src, i):
        there = block(at(STEPS[i], 0))
        send(src, there, B_IN + 3 * i, at(0, TURN[i]))
        send(src, there, B_IN + 3 * i + 1, at(0, -TURN[i]))

    def first_near():
        here = block(at(-1, 0))
        arrived(here, A_IN)
        send(here, here, A_IN + 2, at(1, 0))
        second_out(here, 1)
        swap(here, 1, 0)

    def first_behind():
        here = block(at(1, 0))
        arrived(here, A_IN + 1)
        second_out(here, 2)
        swap(here, 2, 0)

    def first_far():
        here = block(at(2, 0))
        arrived(here, A_IN + 2)
        second_out(here, 3)
        swap(here, 3, 0)

    def second_near(i):
        here = block(at(STEPS[i], -TURN[i]))
        arrived(here, B_IN + 3 * i)
        send(here, here, B_IN + 3 * i + 2, at(0, TURN[i]))
        swap(here, i, STEPS.index(-TURN[i]))

    def second_behind(i):
        here = block(at(STEPS[i], TURN[i]))
        arrived(here, B_IN + 3 * i + 1)
        swap(here, i, STEPS.index(TURN[i]))

    def second_far(i):
        here = block(at(STEPS[i], 2))
        arrived(here, B_IN + 3 * i + 2)
        swap(here, i, 3)

    def swapped(i):
        for j in range(4):
            x, y = mod(cx + STEPS[i], SIDE), mod(cy + STEPS[j], SIDE)
            number = SWAP + (4 * j + i) * (1 - core) + (4 * i + j) * core
            arrived(block((x * SIDE + y) * 2 + 1 - core), number)

    def send_q():
        for r in range(2):
            for g in range(2):
                rows = pl.ds(CHUNK * r, CHUNK)
                send(pre.at[0, rows, pl.ds(2 * D + PIECE * g, PIECE)], piece(qraw, r, g), Q_IN + 2 * r + g, before)

    send_q()
    first_out(w.at[0])
    first_back(w.at[0])
    second_out(w.at[0], 0)
    swap(w.at[0], 0, 0)

    def activate(group, target):
        def step(i, carry):
            rows = pl.ds(pl.multiple_of(i * 32, 32), 32)
            value = pre_v[rows, pl.ds(D * group, D)].astype(F32)
            s = sigmoid(value)
            act = value * s
            target[rows, :] = act.astype(BF16)
            slopes[rows, pl.ds(D * group, D)] = s + act * (1.0 - s)
            return carry

        local[group].wait()
        lax.fori_loop(0, TILE // 32, step, 0)

    def head_columns(h):
        return pl.ds(pl.multiple_of(h * HEAD_DIM, HEAD_DIM), HEAD_DIM)

    def weigh(scores, first_row=None):
        z = scores * SCALE
        s = sigmoid(z)
        p = z * s
        slope = s + p * (1.0 - s)
        if first_row is not None:
            row = lax.broadcasted_iota(jnp.int32, scores.shape, 0) + first_row
            keep = lax.broadcasted_iota(jnp.int32, scores.shape, 1) <= row
            p = jnp.where(keep, p, 0.0)
            slope = jnp.where(keep, slope, 0.0)
        return p.astype(BF16), slope.astype(BF16)

    def same_forward(r):
        keys = CHUNK * (r + 1)

        def step(h, carry):
            cols = head_columns(h)
            p, slope = weigh(dot_nt(qbuf[chunk(r), cols], kbuf[0:keys, cols]), CHUNK * r)
            p_same[h, chunk(r), 0:keys] = p
            s_same[h, chunk(r), 0:keys] = slope
            if keys < TILE:
                p_same[h, chunk(r), keys:TILE] = jnp.zeros((CHUNK, TILE - keys), BF16)
                s_same[h, chunk(r), keys:TILE] = jnp.zeros((CHUNK, TILE - keys), BF16)
            mix[chunk(r), cols] = dot_nn(p, vbuf[0:keys, cols]) * (1.0 / TILE)
            return carry

        lax.fori_loop(0, HEADS, step, 0, unroll=UNROLL)

    def cross_forward(r, g):
        arrived(piece(qraw, r, g), Q_IN + 2 * r + g)
        value = qraw[chunk(r), columns(g)].astype(F32)
        qx[chunk(r), columns(g)] = (value * sigmoid(value)).astype(BF16)

        def step(h, carry):
            cols = head_columns(h)
            p, slope = weigh(dot_nt(qx[chunk(r), cols], kbuf[:, cols]))
            p_cross[h, chunk(r), :] = p
            s_cross[h, chunk(r), :] = slope
            o_stage[chunk(r), cols] = (dot_nn(p, vbuf[:, cols]) * (1.0 / TILE)).astype(BF16)
            return carry

        lax.fori_loop(GROUP * g, GROUP * (g + 1), step, 0, unroll=UNROLL)
        send(piece(o_stage, r, g), piece(oraw, r, g), O_IN + 2 * r + g, after)

    def norm(r):
        for g in range(2):
            arrived(piece(oraw, r, g), O_IN + 2 * r + g)

        def step(i, carry):
            start = CHUNK * r + i * 32
            rows = pl.ds(pl.multiple_of(start, 32), 32)
            mixed = mix[rows, :] + oraw[rows, :].astype(F32) * takes
            centered = mixed - jnp.mean(mixed, axis=-1, keepdims=True)
            inv_std = lax.rsqrt(jnp.mean(centered * centered, axis=-1, keepdims=True) + EPSILON)
            normed = centered * inv_std
            live = lax.broadcasted_iota(jnp.int32, (32, 1), 0) + start < valid
            cot = jnp.where(live, og_v[rows, :].astype(F32), 0.0)
            grads[rows, pl.ds(0, D)] = (cot * normed * slopes[rows, pl.ds(0, D)]).astype(BF16)
            grad_norm = cot * gate_buf[rows, :].astype(F32)
            grad_mix = inv_std * (
                grad_norm
                - jnp.mean(grad_norm, axis=-1, keepdims=True)
                - normed * jnp.mean(grad_norm * normed, axis=-1, keepdims=True)
            )
            dobuf[rows, :] = grad_mix.astype(BF16)
            do_stage[rows, :] = (grad_mix * takes).astype(BF16)
            return carry

        lax.fori_loop(0, CHUNK // 32, step, 0, unroll=UNROLL)
        for g in range(2):
            send(piece(do_stage, r, g), piece(doraw, r, g), DO_IN + 2 * r + g, before)

    def same_backward(r):
        keys = CHUNK * (r + 1)

        def step(h, carry):
            cols = head_columns(h)
            dp = dot_nt(dobuf[chunk(r), cols], vbuf[0:keys, cols])
            ds = (dp * s_same[h, chunk(r), 0:keys].astype(F32)).astype(BF16)
            s_same[h, chunk(r), 0:keys] = ds
            dq_sum[chunk(r), cols] = dot_nn(ds, kbuf[0:keys, cols]) * (SCALE / TILE)
            return carry

        lax.fori_loop(0, HEADS, step, 0, unroll=UNROLL)

    def cross_backward(r, g):
        arrived(piece(doraw, r, g), DO_IN + 2 * r + g)

        def step(h, carry):
            cols = head_columns(h)
            dp = dot_nt(doraw[chunk(r), cols], vbuf[:, cols])
            ds = (dp * s_cross[h, chunk(r), :].astype(F32)).astype(BF16)
            s_cross[h, chunk(r), :] = ds
            dq_stage[chunk(r), cols] = (dot_nn(ds, kbuf[:, cols]) * (SCALE / TILE)).astype(BF16)
            return carry

        lax.fori_loop(GROUP * g, GROUP * (g + 1), step, 0, unroll=UNROLL)
        send(piece(dq_stage, r, g), piece(dqraw, r, g), DQ_IN + 2 * r + g, after)

    def finish_kv(g):
        def step(h, carry):
            cols = head_columns(h)
            dv = (dot_tn(p_same[h], dobuf[:, cols]) + dot_tn(p_cross[h], doraw[:, cols])) * (1.0 / TILE)
            dk = (dot_tn(s_same[h], qbuf[:, cols]) + dot_tn(s_cross[h], qx[:, cols])) * (SCALE / TILE)
            for i, value in ((1, dv), (3, dk)):
                there = pl.ds(pl.multiple_of(D * i + h * HEAD_DIM, HEAD_DIM), HEAD_DIM)
                grads[:, there] = (value * slopes[:, there]).astype(BF16)
            return carry

        lax.fori_loop(GROUP * g, GROUP * (g + 1), step, 0, unroll=UNROLL)

    def finish_q(r, g):
        arrived(piece(dqraw, r, g), DQ_IN + 2 * r + g)
        there = pl.ds(2 * D + PIECE * g, PIECE)
        dq = dq_sum[chunk(r), columns(g)] + dqraw[chunk(r), columns(g)].astype(F32)
        grads[chunk(r), there] = (dq * slopes[chunk(r), there]).astype(BF16)

    def out_copy(i):
        cols = pl.ds(pl.multiple_of(mod(cx + STEPS[i], SIDE) * TILE, TILE), TILE)
        return copy(staged.at[i], out.at[0, :, cols], OUT + i, {"section": mod(section - 1, SECTIONS)})

    def project(i):
        rows = pl.ds(pl.multiple_of(mod(cx + STEPS[i], SIDE) * TILE, TILE), TILE)
        staged[i] = dot_nt(grads[...], wbuf[rows, :]).astype(BF16)

        @pl.when(section > 0)
        def _():
            out_copy(i).start()

    activate(2, qbuf)
    activate(3, kbuf)
    activate(1, vbuf)
    same_forward(0)
    first_near()
    cross_forward(0, 0)
    cross_forward(0, 1)
    first_behind()

    local[6].wait()
    local[7].wait()
    end = jnp.int32(0)
    place = jnp.int32(0)
    total = jnp.int32(0)
    for user in range(DEVICES):
        length = len_ref[0, user]
        begin = end
        end = begin + lax.div(length + (TILE - 1), TILE)
        mine = jnp.logical_and(begin <= me, me < end)
        place = jnp.where(mine, me - begin, place)
        total = jnp.where(mine, length, total)
    valid = jnp.minimum(total - place * TILE, TILE)
    linked = jnp.where(jnp.logical_and(place >= 1, link_ref[0, 0] == 1), 1, 0).astype(jnp.int32)
    takes = linked.astype(F32)

    same_forward(1)
    cross_forward(1, 0)
    cross_forward(1, 1)
    first_far()
    second_near(0)
    activate(0, gate_buf)
    local[4].wait()
    local[5].wait()
    norm(0)
    second_behind(0)
    norm(1)
    second_near(1)
    same_backward(0)
    second_behind(1)
    cross_backward(0, 0)
    cross_backward(0, 1)
    second_near(2)
    same_backward(1)
    second_behind(2)
    cross_backward(1, 0)
    cross_backward(1, 1)
    second_near(3)
    finish_kv(0)
    finish_kv(1)
    for r in range(2):
        for g in range(2):
            finish_q(r, g)
    second_behind(3)
    for i in range(4):
        second_far(i)
        swapped(i)
        project(i)

    for moved in sent:
        moved.wait_send()

    @pl.when(section > 0)
    def _():
        for i in range(4):
            out_copy(i).wait_send()

    @pl.when(section < SECTIONS - 1)
    def _():
        for i in range(4):
            out_copy(i).wait_recv()

    @pl.when(section == SECTIONS - 1)
    def _():
        mix[...] = jnp.zeros_like(mix)
        o_stage[...] = mix[...].astype(BF16)
        zeros = pltpu.make_async_copy(o_stage, out.at[0], local_sem.at[0])
        zeros.start()
        zeros.wait()


def body(pre_act, out_grad, proj_weight, lengths, link_bits):
    wide = pltpu.VMEM((TILE, D), BF16)
    all_columns = pltpu.VMEM((TILE, 4 * D), BF16)
    totals = pltpu.VMEM((TILE, D), F32)
    scores = pltpu.VMEM((HEADS, TILE, TILE), BF16)
    hbm = pl.BlockSpec(memory_space=pltpu.HBM)
    return pl.pallas_call(
        kernel,
        out_shape=jax.ShapeDtypeStruct((1, TILE, D), BF16),
        in_specs=[hbm] * 5,
        out_specs=hbm,
        scratch_shapes=[
            pltpu.SMEM((1, DEVICES), jnp.int32),
            pltpu.SMEM((1, 1), jnp.int32),
            all_columns,
            wide,
            pltpu.VMEM((D, 4 * D), BF16),
            wide, wide, wide, wide,
            pltpu.VMEM((TILE, 4 * D), F32),
            wide, wide, wide, wide, wide, wide, wide, wide, wide,
            scores, scores, scores, scores,
            totals, totals,
            all_columns,
            pltpu.VMEM((SIDE, TILE, TILE), BF16),
            pltpu.SemaphoreType.DMA((TRANSFERS,)),
            pltpu.SemaphoreType.DMA((TRANSFERS,)),
            pltpu.SemaphoreType.DMA((8,)),
        ],
        compiler_params=pltpu.CompilerParams(
            collective_id=0, has_side_effects=True, vmem_limit_bytes=63 * 1024 * 1024
        ),
    )(lengths, link_bits, pre_act, out_grad, proj_weight)


def solution(mesh):
    placed = (
        P("section", "seq", None),
        P("section", "seq", None),
        P("section", "seq", None),
        P("section", None),
        P("section", "seq"),
    )
    return jax.shard_map(
        body, mesh=mesh, in_specs=placed, out_specs=P("section", "seq", None), check_vma=False
    )
```

```python
import jax
import jax.numpy as jnp
from jax import lax
from jax.experimental import pallas as pl
from jax.experimental.pallas import tpu as pltpu
from jax.sharding import PartitionSpec as P

D = 1024
HEADS = 8
HEAD_DIM = 128
TILE = 256
SIDE = 4
SECTIONS = 16
DEVICES = 32
SHARD = D // DEVICES
EPSILON = 1e-05
MESH = pl.DeviceIdType.MESH
F32 = jnp.float32
BF16 = jnp.bfloat16
SCALE = HEAD_DIM ** (-0.5)

CHUNK = 128
PIECE = 512
GROUP = PIECE // HEAD_DIM
UNROLL = 4

STEPS = (0, -1, 1, 2)
TURN = (-1, 1, -1, 1)

A_IN = 0
B_IN = 3
SWAP = 15
Q_IN = 31
O_IN = 35
DO_IN = 39
DQ_IN = 43
OUT = 47
TRANSFERS = 51


def mod(value, size):
    return lax.rem(value + size, size)


def dot_nn(a, b):
    return lax.dot_general(a, b, (((1,), (0,)), ((), ())), preferred_element_type=F32)


def dot_nt(a, b):
    return lax.dot_general(a, b, (((1,), (1,)), ((), ())), preferred_element_type=F32)


def dot_tn(a, b):
    return lax.dot_general(a, b, (((0,), (0,)), ((), ())), preferred_element_type=F32)


def sigmoid(values):
    return 0.5 * jnp.tanh(0.5 * values) + 0.5


def kernel(
    lengths, link_bits, pre, og, w, out,
    len_ref, link_ref, pre_v, og_v, wbuf, kbuf, vbuf, qbuf, gate_buf, slopes,
    qraw, oraw, doraw, dqraw, qx, dobuf, o_stage, do_stage, dq_stage,
    p_same, s_same, p_cross, s_cross, mix, dq_sum, grads, staged,
    send_sem, recv_sem, local_sem,
):
    section = lax.axis_index("section")
    me = lax.axis_index("seq")
    core = lax.rem(me, 2)
    cy = lax.rem(lax.div(me, 2), SIDE)
    cx = lax.div(me, 2 * SIDE)
    other = me + 1 - 2 * core
    after = mod(me + 1, DEVICES)
    before = mod(me - 1, DEVICES)

    def at(a, b):
        x = mod(cx + a * (1 - core) + b * core, SIDE)
        y = mod(cy + a * core + b * (1 - core), SIDE)
        return (x * SIDE + y) * 2 + core

    def block(device):
        return wbuf.at[pl.ds(pl.multiple_of(device * SHARD, SHARD), SHARD)]

    local = [
        pltpu.make_async_copy(pre.at[0, :, pl.ds(D * i, D)], pre_v.at[:, pl.ds(D * i, D)], local_sem.at[i])
        for i in range(4)
    ]
    local.append(pltpu.make_async_copy(og.at[0], og_v, local_sem.at[4]))
    local.append(pltpu.make_async_copy(w.at[0], block(me), local_sem.at[5]))
    local.append(pltpu.make_async_copy(lengths, len_ref, local_sem.at[6]))
    local.append(pltpu.make_async_copy(link_bits, link_ref, local_sem.at[7]))
    barrier = pltpu.get_barrier_semaphore()
    peers = [
        {"seq": other},
        {"seq": at(1, 0)},
        {"seq": at(-1, 0)},
        {"seq": at(0, 1)},
        {"seq": at(0, -1)},
        {"seq": after + (before - after) * (1 - core)},
        {"section": mod(section + 1, SECTIONS)},
        {"section": mod(section - 1, SECTIONS)},
    ]
    for peer in peers:
        pl.semaphore_signal(barrier, inc=1, device_id=peer, device_id_type=MESH)
    for i in (2, 3, 1, 6, 7, 0, 4, 5):
        local[i].start()
    pl.semaphore_wait(barrier, len(peers))

    sent = []

    def copy(src, dst, number, target):
        return pltpu.make_async_remote_copy(
            src_ref=src, dst_ref=dst, send_sem=send_sem.at[number], recv_sem=recv_sem.at[number],
            device_id=target, device_id_type=MESH,
        )

    def send(src, dst, number, target):
        moved = copy(src, dst, number, {"seq": target})
        moved.start()
        sent.append(moved)

    def arrived(dst, number):
        copy(dst, dst, number, {"seq": other}).wait_recv()

    def chunk(r):
        return pl.ds(CHUNK * r, CHUNK)

    def columns(g):
        return pl.ds(PIECE * g, PIECE)

    def piece(ref, r, g):
        return ref.at[chunk(r), columns(g)]

    def swap(src, i, j):
        send(src, block(at(STEPS[i], STEPS[j])), SWAP + 4 * i + j, other)

    def first_out(src):
        send(src, block(me), A_IN, at(1, 0))

    def first_back(src):
        send(src, block(me), A_IN + 1, at(-1, 0))

    def second_out(src, i):
        there = block(at(STEPS[i], 0))
        send(src, there, B_IN + 3 * i, at(0, TURN[i]))
        send(src, there, B_IN + 3 * i + 1, at(0, -TURN[i]))

    def first_near():
        here = block(at(-1, 0))
        arrived(here, A_IN)
        send(here, here, A_IN + 2, at(1, 0))
        second_out(here, 1)
        swap(here, 1, 0)

    def first_behind():
        here = block(at(1, 0))
        arrived(here, A_IN + 1)
        second_out(here, 2)
        swap(here, 2, 0)

    def first_far():
        here = block(at(2, 0))
        arrived(here, A_IN + 2)
        second_out(here, 3)
        swap(here, 3, 0)

    def second_near(i):
        here = block(at(STEPS[i], -TURN[i]))
        arrived(here, B_IN + 3 * i)
        send(here, here, B_IN + 3 * i + 2, at(0, TURN[i]))
        swap(here, i, STEPS.index(-TURN[i]))

    def second_behind(i):
        here = block(at(STEPS[i], TURN[i]))
        arrived(here, B_IN + 3 * i + 1)
        swap(here, i, STEPS.index(TURN[i]))

    def second_far(i):
        here = block(at(STEPS[i], 2))
        arrived(here, B_IN + 3 * i + 2)
        swap(here, i, 3)

    def swapped(i):
        for j in range(4):
            x, y = mod(cx + STEPS[i], SIDE), mod(cy + STEPS[j], SIDE)
            number = SWAP + (4 * j + i) * (1 - core) + (4 * i + j) * core
            arrived(block((x * SIDE + y) * 2 + 1 - core), number)

    def send_q():
        for r in range(2):
            for g in range(2):
                rows = pl.ds(CHUNK * r, CHUNK)
                send(pre.at[0, rows, pl.ds(2 * D + PIECE * g, PIECE)], piece(qraw, r, g), Q_IN + 2 * r + g, before)

    send_q()
    first_out(w.at[0])
    first_back(w.at[0])
    second_out(w.at[0], 0)
    swap(w.at[0], 0, 0)

    def activate(group, target):
        def step(i, carry):
            rows = pl.ds(pl.multiple_of(i * 32, 32), 32)
            value = pre_v[rows, pl.ds(D * group, D)].astype(F32)
            s = sigmoid(value)
            act = value * s
            target[rows, :] = act.astype(BF16)
            slopes[rows, pl.ds(D * group, D)] = s + act * (1.0 - s)
            return carry

        local[group].wait()
        lax.fori_loop(0, TILE // 32, step, 0)

    def head_columns(h):
        return pl.ds(pl.multiple_of(h * HEAD_DIM, HEAD_DIM), HEAD_DIM)

    def weigh(scores, first_row=None):
        z = scores * SCALE
        s = sigmoid(z)
        p = z * s
        slope = s + p * (1.0 - s)
        if first_row is not None:
            row = lax.broadcasted_iota(jnp.int32, scores.shape, 0) + first_row
            keep = lax.broadcasted_iota(jnp.int32, scores.shape, 1) <= row
            p = jnp.where(keep, p, 0.0)
            slope = jnp.where(keep, slope, 0.0)
        return p.astype(BF16), slope.astype(BF16)

    def same_forward(r):
        keys = CHUNK * (r + 1)

        def step(h, carry):
            cols = head_columns(h)
            p, slope = weigh(dot_nt(qbuf[chunk(r), cols], kbuf[0:keys, cols]), CHUNK * r)
            p_same[h, chunk(r), 0:keys] = p
            s_same[h, chunk(r), 0:keys] = slope
            if keys < TILE:
                p_same[h, chunk(r), keys:TILE] = jnp.zeros((CHUNK, TILE - keys), BF16)
                s_same[h, chunk(r), keys:TILE] = jnp.zeros((CHUNK, TILE - keys), BF16)
            mix[chunk(r), cols] = dot_nn(p, vbuf[0:keys, cols]) * (1.0 / TILE)
            return carry

        lax.fori_loop(0, HEADS, step, 0, unroll=UNROLL)

    def cross_forward(r, g):
        arrived(piece(qraw, r, g), Q_IN + 2 * r + g)
        value = qraw[chunk(r), columns(g)].astype(F32)
        qx[chunk(r), columns(g)] = (value * sigmoid(value)).astype(BF16)

        def step(h, carry):
            cols = head_columns(h)
            p, slope = weigh(dot_nt(qx[chunk(r), cols], kbuf[:, cols]))
            p_cross[h, chunk(r), :] = p
            s_cross[h, chunk(r), :] = slope
            o_stage[chunk(r), cols] = (dot_nn(p, vbuf[:, cols]) * (1.0 / TILE)).astype(BF16)
            return carry

        lax.fori_loop(GROUP * g, GROUP * (g + 1), step, 0, unroll=UNROLL)
        send(piece(o_stage, r, g), piece(oraw, r, g), O_IN + 2 * r + g, after)

    def norm(r):
        for g in range(2):
            arrived(piece(oraw, r, g), O_IN + 2 * r + g)

        def step(i, carry):
            start = CHUNK * r + i * 32
            rows = pl.ds(pl.multiple_of(start, 32), 32)
            mixed = mix[rows, :] + oraw[rows, :].astype(F32) * takes
            centered = mixed - jnp.mean(mixed, axis=-1, keepdims=True)
            inv_std = lax.rsqrt(jnp.mean(centered * centered, axis=-1, keepdims=True) + EPSILON)
            normed = centered * inv_std
            live = lax.broadcasted_iota(jnp.int32, (32, 1), 0) + start < valid
            cot = jnp.where(live, og_v[rows, :].astype(F32), 0.0)
            grads[rows, pl.ds(0, D)] = (cot * normed * slopes[rows, pl.ds(0, D)]).astype(BF16)
            grad_norm = cot * gate_buf[rows, :].astype(F32)
            grad_mix = inv_std * (
                grad_norm
                - jnp.mean(grad_norm, axis=-1, keepdims=True)
                - normed * jnp.mean(grad_norm * normed, axis=-1, keepdims=True)
            )
            dobuf[rows, :] = grad_mix.astype(BF16)
            do_stage[rows, :] = (grad_mix * takes).astype(BF16)
            return carry

        lax.fori_loop(0, CHUNK // 32, step, 0, unroll=UNROLL)
        for g in range(2):
            send(piece(do_stage, r, g), piece(doraw, r, g), DO_IN + 2 * r + g, before)

    def same_backward(r):
        keys = CHUNK * (r + 1)

        def step(h, carry):
            cols = head_columns(h)
            dp = dot_nt(dobuf[chunk(r), cols], vbuf[0:keys, cols])
            ds = (dp * s_same[h, chunk(r), 0:keys].astype(F32)).astype(BF16)
            s_same[h, chunk(r), 0:keys] = ds
            dq_sum[chunk(r), cols] = dot_nn(ds, kbuf[0:keys, cols]) * (SCALE / TILE)
            return carry

        lax.fori_loop(0, HEADS, step, 0, unroll=UNROLL)

    def cross_backward(r, g):
        arrived(piece(doraw, r, g), DO_IN + 2 * r + g)

        def step(h, carry):
            cols = head_columns(h)
            dp = dot_nt(doraw[chunk(r), cols], vbuf[:, cols])
            ds = (dp * s_cross[h, chunk(r), :].astype(F32)).astype(BF16)
            s_cross[h, chunk(r), :] = ds
            dq_stage[chunk(r), cols] = (dot_nn(ds, kbuf[:, cols]) * (SCALE / TILE)).astype(BF16)
            return carry

        lax.fori_loop(GROUP * g, GROUP * (g + 1), step, 0, unroll=UNROLL)
        send(piece(dq_stage, r, g), piece(dqraw, r, g), DQ_IN + 2 * r + g, after)

    def finish_kv(g):
        def step(h, carry):
            cols = head_columns(h)
            dv = (dot_tn(p_same[h], dobuf[:, cols]) + dot_tn(p_cross[h], doraw[:, cols])) * (1.0 / TILE)
            dk = (dot_tn(s_same[h], qbuf[:, cols]) + dot_tn(s_cross[h], qx[:, cols])) * (SCALE / TILE)
            for i, value in ((1, dv), (3, dk)):
                there = pl.ds(pl.multiple_of(D * i + h * HEAD_DIM, HEAD_DIM), HEAD_DIM)
                grads[:, there] = (value * slopes[:, there]).astype(BF16)
            return carry

        lax.fori_loop(GROUP * g, GROUP * (g + 1), step, 0, unroll=UNROLL)

    def finish_q(r, g):
        arrived(piece(dqraw, r, g), DQ_IN + 2 * r + g)
        there = pl.ds(2 * D + PIECE * g, PIECE)
        dq = dq_sum[chunk(r), columns(g)] + dqraw[chunk(r), columns(g)].astype(F32)
        grads[chunk(r), there] = (dq * slopes[chunk(r), there]).astype(BF16)

    def out_copy(i):
        cols = pl.ds(pl.multiple_of(mod(cx + STEPS[i], SIDE) * TILE, TILE), TILE)
        return copy(staged.at[i], out.at[0, :, cols], OUT + i, {"section": mod(section - 1, SECTIONS)})

    def project(i):
        rows = pl.ds(pl.multiple_of(mod(cx + STEPS[i], SIDE) * TILE, TILE), TILE)
        staged[i] = dot_nt(grads[...], wbuf[rows, :]).astype(BF16)

        @pl.when(section > 0)
        def _():
            out_copy(i).start()

    activate(2, qbuf)
    activate(3, kbuf)
    activate(1, vbuf)
    same_forward(0)
    first_near()
    cross_forward(0, 0)
    cross_forward(0, 1)
    first_behind()

    local[6].wait()
    local[7].wait()
    end = jnp.int32(0)
    place = jnp.int32(0)
    total = jnp.int32(0)
    for user in range(DEVICES):
        length = len_ref[0, user]
        begin = end
        end = begin + lax.div(length + (TILE - 1), TILE)
        mine = jnp.logical_and(begin <= me, me < end)
        place = jnp.where(mine, me - begin, place)
        total = jnp.where(mine, length, total)
    valid = jnp.minimum(total - place * TILE, TILE)
    linked = jnp.where(jnp.logical_and(place >= 1, link_ref[0, 0] == 1), 1, 0).astype(jnp.int32)
    takes = linked.astype(F32)

    same_forward(1)
    cross_forward(1, 0)
    cross_forward(1, 1)
    first_far()
    second_near(0)
    activate(0, gate_buf)
    local[4].wait()
    local[5].wait()
    norm(0)
    second_behind(0)
    norm(1)
    second_near(1)
    same_backward(0)
    second_behind(1)
    cross_backward(0, 0)
    cross_backward(0, 1)
    second_near(2)
    same_backward(1)
    second_behind(2)
    cross_backward(1, 0)
    cross_backward(1, 1)
    second_near(3)
    finish_kv(0)
    finish_kv(1)
    for r in range(2):
        for g in range(2):
            finish_q(r, g)
    second_behind(3)
    for i in range(4):
        second_far(i)
        swapped(i)
        project(i)

    for moved in sent:
        moved.wait_send()

    @pl.when(section > 0)
    def _():
        for i in range(4):
            out_copy(i).wait_send()

    @pl.when(section < SECTIONS - 1)
    def _():
        for i in range(4):
            out_copy(i).wait_recv()

    @pl.when(section == SECTIONS - 1)
    def _():
        mix[...] = jnp.zeros_like(mix)
        o_stage[...] = mix[...].astype(BF16)
        zeros = pltpu.make_async_copy(o_stage, out.at[0], local_sem.at[0])
        zeros.start()
        zeros.wait()


def body(pre_act, out_grad, proj_weight, lengths, link_bits):
    wide = pltpu.VMEM((TILE, D), BF16)
    all_columns = pltpu.VMEM((TILE, 4 * D), BF16)
    totals = pltpu.VMEM((TILE, D), F32)
    scores = pltpu.VMEM((HEADS, TILE, TILE), BF16)
    hbm = pl.BlockSpec(memory_space=pltpu.HBM)
    return pl.pallas_call(
        kernel,
        out_shape=pltpu.VMEM((1, TILE, D), BF16),
        in_specs=[hbm] * 5,
        out_specs=pl.BlockSpec(memory_space=pl.ANY),
        scratch_shapes=[
            pltpu.SMEM((1, DEVICES), jnp.int32),
            pltpu.SMEM((1, 1), jnp.int32),
            all_columns,
            wide,
            pltpu.VMEM((D, 4 * D), BF16),
            wide, wide, wide, wide,
            pltpu.VMEM((TILE, 4 * D), F32),
            wide, wide, wide, wide, wide, wide, wide, wide, wide,
            scores, scores, scores, scores,
            totals, totals,
            all_columns,
            pltpu.VMEM((SIDE, TILE, TILE), BF16),
            pltpu.SemaphoreType.DMA((TRANSFERS,)),
            pltpu.SemaphoreType.DMA((TRANSFERS,)),
            pltpu.SemaphoreType.DMA((8,)),
        ],
        compiler_params=pltpu.CompilerParams(
            collective_id=0, has_side_effects=True, vmem_limit_bytes=63 * 1024 * 1024
        ),
    )(lengths, link_bits, pre_act, out_grad, proj_weight)


def solution(mesh):
    placed = (
        P("section", "seq", None),
        P("section", "seq", None),
        P("section", "seq", None),
        P("section", None),
        P("section", "seq"),
    )
    return jax.shard_map(
        body, mesh=mesh, in_specs=placed, out_specs=P("section", "seq", None), check_vma=False
    )
```

```python
import jax
import jax.numpy as jnp
from jax import lax
from jax.experimental import pallas as pl
from jax.experimental.pallas import tpu as pltpu
from jax.sharding import PartitionSpec as P

D = 1024
HEADS = 8
HEAD_DIM = 128
TILE = 256
SIDE = 4
SECTIONS = 16
DEVICES = 32
SHARD = D // DEVICES
EPSILON = 1e-05
MESH = pl.DeviceIdType.MESH
F32 = jnp.float32
BF16 = jnp.bfloat16
SCALE = HEAD_DIM ** (-0.5)

CHUNK = 128
PIECE = 512
GROUP = PIECE // HEAD_DIM
UNROLL = 4

STEPS = (0, -1, 1, 2)
TURN = (-1, 1, -1, 1)

A_IN = 0
B_IN = 3
SWAP = 15
Q_IN = 31
O_IN = 35
DO_IN = 39
DQ_IN = 43
OUT = 47
TRANSFERS = 52


def mod(value, size):
    return lax.rem(value + size, size)


def dot_nn(a, b):
    return lax.dot_general(a, b, (((1,), (0,)), ((), ())), preferred_element_type=F32)


def dot_nt(a, b):
    return lax.dot_general(a, b, (((1,), (1,)), ((), ())), preferred_element_type=F32)


def dot_tn(a, b):
    return lax.dot_general(a, b, (((0,), (0,)), ((), ())), preferred_element_type=F32)


def sigmoid(values):
    return 0.5 * jnp.tanh(0.5 * values) + 0.5


def kernel(
    lengths, link_bits, pre, og, w, out,
    len_ref, link_ref, pre_v, og_v, wbuf, kbuf, vbuf, qbuf, gate_buf, slopes,
    qraw, oraw, doraw, dqraw, qx, dobuf, o_stage, do_stage, dq_stage,
    p_same, s_same, p_cross, s_cross, mix, dq_sum, grads, staged,
    send_sem, recv_sem, local_sem,
):
    section = lax.axis_index("section")
    me = lax.axis_index("seq")
    core = lax.rem(me, 2)
    cy = lax.rem(lax.div(me, 2), SIDE)
    cx = lax.div(me, 2 * SIDE)
    other = me + 1 - 2 * core
    after = mod(me + 1, DEVICES)
    before = mod(me - 1, DEVICES)

    def at(a, b):
        x = mod(cx + a * (1 - core) + b * core, SIDE)
        y = mod(cy + a * core + b * (1 - core), SIDE)
        return (x * SIDE + y) * 2 + core

    def block(device):
        return wbuf.at[pl.ds(pl.multiple_of(device * SHARD, SHARD), SHARD)]

    local = [
        pltpu.make_async_copy(pre.at[0, :, pl.ds(D * i, D)], pre_v.at[:, pl.ds(D * i, D)], local_sem.at[i])
        for i in range(4)
    ]
    local.append(pltpu.make_async_copy(og.at[0], og_v, local_sem.at[4]))
    local.append(pltpu.make_async_copy(w.at[0], block(me), local_sem.at[5]))
    local.append(pltpu.make_async_copy(lengths, len_ref, local_sem.at[6]))
    local.append(pltpu.make_async_copy(link_bits, link_ref, local_sem.at[7]))
    barrier = pltpu.get_barrier_semaphore()
    peers = [
        {"seq": other},
        {"seq": at(1, 0)},
        {"seq": at(-1, 0)},
        {"seq": at(0, 1)},
        {"seq": at(0, -1)},
        {"seq": after + (before - after) * (1 - core)},
        {"section": mod(section + 1, SECTIONS)},
        {"section": mod(section - 1, SECTIONS)},
    ]
    for peer in peers:
        pl.semaphore_signal(barrier, inc=1, device_id=peer, device_id_type=MESH)
    for i in (2, 3, 1, 6, 7, 0, 4, 5):
        local[i].start()
    pl.semaphore_wait(barrier, len(peers))

    sent = []

    def copy(src, dst, number, target):
        return pltpu.make_async_remote_copy(
            src_ref=src, dst_ref=dst, send_sem=send_sem.at[number], recv_sem=recv_sem.at[number],
            device_id=target, device_id_type=MESH,
        )

    def send(src, dst, number, target):
        moved = copy(src, dst, number, {"seq": target})
        moved.start()
        sent.append(number)

    def arrived(dst, number):
        copy(dst, dst, number, {"seq": other}).wait_recv()

    def chunk(r):
        return pl.ds(CHUNK * r, CHUNK)

    def columns(g):
        return pl.ds(PIECE * g, PIECE)

    def piece(ref, r, g):
        return ref.at[chunk(r), columns(g)]

    def swap(src, i, j):
        send(src, block(at(STEPS[i], STEPS[j])), SWAP + 4 * i + j, other)

    def first_out():
        send(w.at[0], block(me), A_IN, at(1, 0))

    def first_back():
        send(w.at[0], block(me), A_IN + 1, at(-1, 0))

    def along(i):
        src, there = w.at[0] if i == 0 else block(at(STEPS[i], 0)), block(at(STEPS[i], 0))
        send(src, there, B_IN + 3 * i, at(0, TURN[i]))

    def against(i):
        src, there = w.at[0] if i == 0 else block(at(STEPS[i], 0)), block(at(STEPS[i], 0))
        send(src, there, B_IN + 3 * i + 1, at(0, -TURN[i]))

    def first_near():
        here = block(at(-1, 0))
        arrived(here, A_IN)
        send(here, here, A_IN + 2, at(1, 0))
        swap(here, 1, 0)

    def first_behind():
        here = block(at(1, 0))
        arrived(here, A_IN + 1)
        swap(here, 2, 0)

    def first_far():
        here = block(at(2, 0))
        arrived(here, A_IN + 2)
        swap(here, 3, 0)

    def second_near(i):
        here = block(at(STEPS[i], -TURN[i]))
        arrived(here, B_IN + 3 * i)
        send(here, here, B_IN + 3 * i + 2, at(0, TURN[i]))
        swap(here, i, STEPS.index(-TURN[i]))

    def second_behind(i):
        here = block(at(STEPS[i], TURN[i]))
        arrived(here, B_IN + 3 * i + 1)
        swap(here, i, STEPS.index(TURN[i]))

    def second_far(i):
        here = block(at(STEPS[i], 2))
        arrived(here, B_IN + 3 * i + 2)
        swap(here, i, 3)

    def swapped(i, ys=STEPS):
        for step in ys:
            j = STEPS.index(step) if isinstance(step, int) else 1 + lax.div(step + 1, 2)
            x, y = mod(cx + STEPS[i], SIDE), mod(cy + step, SIDE)
            number = SWAP + (4 * j + i) * (1 - core) + (4 * i + j) * core
            arrived(block((x * SIDE + y) * 2 + 1 - core), number)

    def send_q():
        for r in range(2):
            for g in range(2):
                rows = pl.ds(CHUNK * r, CHUNK)
                send(pre.at[0, rows, pl.ds(2 * D + PIECE * g, PIECE)], piece(qraw, r, g), Q_IN + 2 * r + g, before)

    send_q()
    first_out()
    first_back()
    swap(w.at[0], 0, 0)
    along(0)
    against(0)

    def activate(group, target):
        def step(i, carry):
            rows = pl.ds(pl.multiple_of(i * 32, 32), 32)
            value = pre_v[rows, pl.ds(D * group, D)].astype(F32)
            s = sigmoid(value)
            act = value * s
            target[rows, :] = act.astype(BF16)
            slopes[rows, pl.ds(D * group, D)] = s + act * (1.0 - s)
            return carry

        local[group].wait()
        lax.fori_loop(0, TILE // 32, step, 0)

    def head_columns(h):
        return pl.ds(pl.multiple_of(h * HEAD_DIM, HEAD_DIM), HEAD_DIM)

    def weigh(scores, first_row=None):
        z = scores * SCALE
        s = sigmoid(z)
        p = z * s
        slope = s + p * (1.0 - s)
        if first_row is not None:
            row = lax.broadcasted_iota(jnp.int32, scores.shape, 0) + first_row
            keep = lax.broadcasted_iota(jnp.int32, scores.shape, 1) <= row
            p = jnp.where(keep, p, 0.0)
            slope = jnp.where(keep, slope, 0.0)
        return p.astype(BF16), slope.astype(BF16)

    def same_forward(r):
        keys = CHUNK * (r + 1)

        def step(h, carry):
            cols = head_columns(h)
            p, slope = weigh(dot_nt(qbuf[chunk(r), cols], kbuf[0:keys, cols]), CHUNK * r)
            p_same[h, chunk(r), 0:keys] = p
            s_same[h, chunk(r), 0:keys] = slope
            if keys < TILE:
                p_same[h, chunk(r), keys:TILE] = jnp.zeros((CHUNK, TILE - keys), BF16)
                s_same[h, chunk(r), keys:TILE] = jnp.zeros((CHUNK, TILE - keys), BF16)
            mix[chunk(r), cols] = dot_nn(p, vbuf[0:keys, cols]) * (1.0 / TILE)
            return carry

        lax.fori_loop(0, HEADS, step, 0, unroll=UNROLL)

    def cross_forward(r, g):
        arrived(piece(qraw, r, g), Q_IN + 2 * r + g)
        value = qraw[chunk(r), columns(g)].astype(F32)
        qx[chunk(r), columns(g)] = (value * sigmoid(value)).astype(BF16)

        def step(h, carry):
            cols = head_columns(h)
            p, slope = weigh(dot_nt(qx[chunk(r), cols], kbuf[:, cols]))
            p_cross[h, chunk(r), :] = p
            s_cross[h, chunk(r), :] = slope
            o_stage[chunk(r), cols] = (dot_nn(p, vbuf[:, cols]) * (1.0 / TILE)).astype(BF16)
            return carry

        lax.fori_loop(GROUP * g, GROUP * (g + 1), step, 0, unroll=UNROLL)
        send(piece(o_stage, r, g), piece(oraw, r, g), O_IN + 2 * r + g, after)

    def norm(r):
        for g in range(2):
            arrived(piece(oraw, r, g), O_IN + 2 * r + g)

        def step(i, carry):
            start = CHUNK * r + i * 32
            rows = pl.ds(pl.multiple_of(start, 32), 32)
            mixed = mix[rows, :] + oraw[rows, :].astype(F32) * takes
            centered = mixed - jnp.mean(mixed, axis=-1, keepdims=True)
            inv_std = lax.rsqrt(jnp.mean(centered * centered, axis=-1, keepdims=True) + EPSILON)
            normed = centered * inv_std
            live = lax.broadcasted_iota(jnp.int32, (32, 1), 0) + start < valid
            cot = jnp.where(live, og_v[rows, :].astype(F32), 0.0)
            grads[rows, pl.ds(0, D)] = (cot * normed * slopes[rows, pl.ds(0, D)]).astype(BF16)
            grad_norm = cot * gate_buf[rows, :].astype(F32)
            grad_mix = inv_std * (
                grad_norm
                - jnp.mean(grad_norm, axis=-1, keepdims=True)
                - normed * jnp.mean(grad_norm * normed, axis=-1, keepdims=True)
            )
            dobuf[rows, :] = grad_mix.astype(BF16)
            do_stage[rows, :] = (grad_mix * takes).astype(BF16)
            return carry

        lax.fori_loop(0, CHUNK // 32, step, 0, unroll=UNROLL)
        for g in range(2):
            send(piece(do_stage, r, g), piece(doraw, r, g), DO_IN + 2 * r + g, before)

    def same_backward(r):
        keys = CHUNK * (r + 1)

        def step(h, carry):
            cols = head_columns(h)
            dp = dot_nt(dobuf[chunk(r), cols], vbuf[0:keys, cols])
            ds = (dp * s_same[h, chunk(r), 0:keys].astype(F32)).astype(BF16)
            s_same[h, chunk(r), 0:keys] = ds
            dq_sum[chunk(r), cols] = dot_nn(ds, kbuf[0:keys, cols]) * (SCALE / TILE)
            return carry

        lax.fori_loop(0, HEADS, step, 0, unroll=UNROLL)

    def cross_backward(r, g):
        arrived(piece(doraw, r, g), DO_IN + 2 * r + g)

        def step(h, carry):
            cols = head_columns(h)
            dp = dot_nt(doraw[chunk(r), cols], vbuf[:, cols])
            ds = (dp * s_cross[h, chunk(r), :].astype(F32)).astype(BF16)
            s_cross[h, chunk(r), :] = ds
            dq_stage[chunk(r), cols] = (dot_nn(ds, kbuf[:, cols]) * (SCALE / TILE)).astype(BF16)
            return carry

        lax.fori_loop(GROUP * g, GROUP * (g + 1), step, 0, unroll=UNROLL)
        send(piece(dq_stage, r, g), piece(dqraw, r, g), DQ_IN + 2 * r + g, after)

    def finish_kv(g):
        def step(h, carry):
            cols = head_columns(h)
            dv = (dot_tn(p_same[h], dobuf[:, cols]) + dot_tn(p_cross[h], doraw[:, cols])) * (1.0 / TILE)
            dk = (dot_tn(s_same[h], qbuf[:, cols]) + dot_tn(s_cross[h], qx[:, cols])) * (SCALE / TILE)
            for i, value in ((1, dv), (3, dk)):
                there = pl.ds(pl.multiple_of(D * i + h * HEAD_DIM, HEAD_DIM), HEAD_DIM)
                grads[:, there] = (value * slopes[:, there]).astype(BF16)
            return carry

        lax.fori_loop(GROUP * g, GROUP * (g + 1), step, 0, unroll=UNROLL)

    def finish_q(r, g):
        arrived(piece(dqraw, r, g), DQ_IN + 2 * r + g)
        there = pl.ds(2 * D + PIECE * g, PIECE)
        dq = dq_sum[chunk(r), columns(g)] + dqraw[chunk(r), columns(g)].astype(F32)
        grads[chunk(r), there] = (dq * slopes[chunk(r), there]).astype(BF16)

    def out_copy(i, half=None, number_of=0):
        start, size = mod(cx + STEPS[i], SIDE) * TILE, TILE
        src, number = staged.at[i], OUT + i
        if half is not None:
            start, size = start + half * CHUNK, CHUNK
            src, number = staged.at[i, :, pl.ds(pl.multiple_of(half * CHUNK, CHUNK), CHUNK)], OUT + i + number_of
        cols = pl.ds(pl.multiple_of(start, CHUNK), size)
        return copy(src, out.at[0, :, cols], number, {"section": mod(section - 1, SECTIONS)})

    def project(i):
        rows = pl.ds(pl.multiple_of(mod(cx + STEPS[i], SIDE) * TILE, TILE), TILE)
        staged[i] = dot_nt(grads[...], wbuf[rows, :]).astype(BF16)

        @pl.when(section > 0)
        def _():
            out_copy(i).start()

    near_half = lax.div(cy, 2)
    beside = 1 - 2 * lax.rem(cy, 2)

    def project_half(half, number_of):
        start = mod(cx + STEPS[3], SIDE) * TILE + half * CHUNK
        rows = pl.ds(pl.multiple_of(start, CHUNK), CHUNK)
        cols = pl.ds(pl.multiple_of(half * CHUNK, CHUNK), CHUNK)
        staged[3, :, cols] = dot_nt(grads[...], wbuf[rows, :]).astype(BF16)

        @pl.when(section > 0)
        def _():
            out_copy(3, half, number_of).start()

    activate(2, qbuf)
    activate(3, kbuf)
    activate(1, vbuf)
    same_forward(0)
    first_near()
    along(1)
    against(1)
    cross_forward(0, 0)
    cross_forward(0, 1)
    first_behind()
    along(2)
    against(2)

    local[6].wait()
    local[7].wait()
    end = jnp.int32(0)
    place = jnp.int32(0)
    total = jnp.int32(0)
    for user in range(DEVICES):
        length = len_ref[0, user]
        begin = end
        end = begin + lax.div(length + (TILE - 1), TILE)
        mine = jnp.logical_and(begin <= me, me < end)
        place = jnp.where(mine, me - begin, place)
        total = jnp.where(mine, length, total)
    valid = jnp.minimum(total - place * TILE, TILE)
    linked = jnp.where(jnp.logical_and(place >= 1, link_ref[0, 0] == 1), 1, 0).astype(jnp.int32)
    takes = linked.astype(F32)

    same_forward(1)
    cross_forward(1, 0)
    cross_forward(1, 1)
    first_far()
    along(3)
    against(3)
    second_near(0)
    activate(0, gate_buf)
    local[4].wait()
    local[5].wait()
    norm(0)
    second_behind(0)
    norm(1)
    second_near(1)
    same_backward(0)
    second_behind(1)
    cross_backward(0, 0)
    cross_backward(0, 1)
    second_near(2)
    same_backward(1)
    second_behind(2)
    cross_backward(1, 0)
    cross_backward(1, 1)
    second_near(3)
    second_far(0)
    finish_kv(0)
    finish_kv(1)
    second_far(1)
    for r in range(2):
        for g in range(2):
            finish_q(r, g)
    second_behind(3)
    second_far(2)
    for i in range(3):
        swapped(i)
        project(i)
    swapped(3, (0, beside))
    project_half(near_half, 0)
    second_far(3)
    swapped(3, (-beside, 2))
    project_half(1 - near_half, 1)

    for number in sent:
        moved = piece(o_stage, 0, 0) if number >= Q_IN else block(0)
        copy(moved, moved, number, {"seq": other}).wait_send()

    @pl.when(section > 0)
    def _():
        for i in range(3):
            out_copy(i).wait_send()
        out_copy(3, near_half, 0).wait_send()
        out_copy(3, 1 - near_half, 1).wait_send()

    @pl.when(section < SECTIONS - 1)
    def _():
        for i in range(3):
            out_copy(i).wait_recv()
        out_copy(3, near_half, 0).wait_recv()
        out_copy(3, 1 - near_half, 1).wait_recv()

    @pl.when(section == SECTIONS - 1)
    def _():
        mix[...] = jnp.zeros_like(mix)
        o_stage[...] = mix[...].astype(BF16)
        zeros = pltpu.make_async_copy(o_stage, out.at[0], local_sem.at[0])
        zeros.start()
        zeros.wait()


def body(pre_act, out_grad, proj_weight, lengths, link_bits):
    wide = pltpu.VMEM((TILE, D), BF16)
    all_columns = pltpu.VMEM((TILE, 4 * D), BF16)
    totals = pltpu.VMEM((TILE, D), F32)
    scores = pltpu.VMEM((HEADS, TILE, TILE), BF16)
    hbm = pl.BlockSpec(memory_space=pltpu.HBM)
    return pl.pallas_call(
        kernel,
        out_shape=pltpu.VMEM((1, TILE, D), BF16),
        in_specs=[hbm] * 5,
        out_specs=pl.BlockSpec(memory_space=pl.ANY),
        scratch_shapes=[
            pltpu.SMEM((1, DEVICES), jnp.int32),
            pltpu.SMEM((1, 1), jnp.int32),
            all_columns,
            wide,
            pltpu.VMEM((D, 4 * D), BF16),
            wide, wide, wide, wide,
            pltpu.VMEM((TILE, 4 * D), F32),
            wide, wide, wide, wide, wide, wide, wide, wide, wide,
            scores, scores, scores, scores,
            totals, totals,
            all_columns,
            pltpu.VMEM((SIDE, TILE, TILE), BF16),
            pltpu.SemaphoreType.DMA((TRANSFERS,)),
            pltpu.SemaphoreType.DMA((TRANSFERS,)),
            pltpu.SemaphoreType.DMA((8,)),
        ],
        compiler_params=pltpu.CompilerParams(
            collective_id=0, has_side_effects=True, vmem_limit_bytes=63 * 1024 * 1024
        ),
    )(lengths, link_bits, pre_act, out_grad, proj_weight)


def solution(mesh):
    placed = (
        P("section", "seq", None),
        P("section", "seq", None),
        P("section", "seq", None),
        P("section", None),
        P("section", "seq"),
    )
    return jax.shard_map(
        body, mesh=mesh, in_specs=placed, out_specs=P("section", "seq", None), check_vma=False
    )
```

```python
import jax
import jax.numpy as jnp
from jax import lax
from jax.experimental import pallas as pl
from jax.experimental.pallas import tpu as pltpu
from jax.sharding import PartitionSpec as P

D = 1024
HEADS = 8
HEAD_DIM = 128
TILE = 256
SIDE = 4
SECTIONS = 16
DEVICES = 32
SHARD = D // DEVICES
EPSILON = 1e-05
MESH = pl.DeviceIdType.MESH
F32 = jnp.float32
BF16 = jnp.bfloat16
SCALE = HEAD_DIM ** (-0.5)

CHUNK = 128
PIECE = 512
GROUP = PIECE // HEAD_DIM
UNROLL = 4

STEPS = (0, -1, 1, 2)
TURN = (-1, 1, -1, 1)

A_IN = 0
B_IN = 3
SWAP = 15
Q_IN = 31
O_IN = 35
DO_IN = 39
DQ_IN = 43
OUT = 47
TRANSFERS = 52


def mod(value, size):
    return lax.rem(value + size, size)


def dot_nn(a, b):
    return lax.dot_general(a, b, (((1,), (0,)), ((), ())), preferred_element_type=F32)


def dot_nt(a, b):
    return lax.dot_general(a, b, (((1,), (1,)), ((), ())), preferred_element_type=F32)


def dot_tn(a, b):
    return lax.dot_general(a, b, (((0,), (0,)), ((), ())), preferred_element_type=F32)


def sigmoid(values):
    return 0.5 * jnp.tanh(0.5 * values) + 0.5


def kernel(
    lengths, link_bits, pre, og, w, out,
    len_ref, link_ref, pre_v, og_v, wbuf, kbuf, vbuf, qbuf, gate_buf, slopes,
    qraw, oraw, doraw, dqraw, qx, dobuf, o_stage, do_stage, dq_stage,
    p_same, s_same, p_cross, s_cross, mix, dq_sum, grads, staged,
    send_sem, recv_sem, local_sem,
):
    section = lax.axis_index("section")
    me = lax.axis_index("seq")
    core = lax.rem(me, 2)
    cy = lax.rem(lax.div(me, 2), SIDE)
    cx = lax.div(me, 2 * SIDE)
    other = me + 1 - 2 * core
    after = mod(me + 1, DEVICES)
    before = mod(me - 1, DEVICES)

    def at(a, b):
        x = mod(cx + a * (1 - core) + b * core, SIDE)
        y = mod(cy + a * core + b * (1 - core), SIDE)
        return (x * SIDE + y) * 2 + core

    def block(device):
        return wbuf.at[pl.ds(pl.multiple_of(device * SHARD, SHARD), SHARD)]

    local = [
        pltpu.make_async_copy(pre.at[0, :, pl.ds(D * i, D)], pre_v.at[:, pl.ds(D * i, D)], local_sem.at[i])
        for i in range(4)
    ]
    local.append(pltpu.make_async_copy(og.at[0], og_v, local_sem.at[4]))
    local.append(pltpu.make_async_copy(w.at[0], block(me), local_sem.at[5]))
    local.append(pltpu.make_async_copy(lengths, len_ref, local_sem.at[6]))
    local.append(pltpu.make_async_copy(link_bits, link_ref, local_sem.at[7]))
    barrier = pltpu.get_barrier_semaphore()
    peers = [
        {"seq": other},
        {"seq": at(1, 0)},
        {"seq": at(-1, 0)},
        {"seq": at(0, 1)},
        {"seq": at(0, -1)},
        {"seq": after + (before - after) * (1 - core)},
        {"section": mod(section + 1, SECTIONS)},
        {"section": mod(section - 1, SECTIONS)},
    ]
    for peer in peers:
        pl.semaphore_signal(barrier, inc=1, device_id=peer, device_id_type=MESH)
    for i in (2, 3, 1, 6, 7, 0, 4, 5):
        local[i].start()
    pl.semaphore_wait(barrier, len(peers))

    sent = []

    def copy(src, dst, number, target):
        return pltpu.make_async_remote_copy(
            src_ref=src, dst_ref=dst, send_sem=send_sem.at[number], recv_sem=recv_sem.at[number],
            device_id=target, device_id_type=MESH,
        )

    def send(src, dst, number, target):
        moved = copy(src, dst, number, {"seq": target})
        moved.start()
        sent.append(number)

    def arrived(dst, number):
        copy(dst, dst, number, {"seq": other}).wait_recv()

    def chunk(r):
        return pl.ds(CHUNK * r, CHUNK)

    def columns(g):
        return pl.ds(PIECE * g, PIECE)

    def piece(ref, r, g):
        return ref.at[chunk(r), columns(g)]

    def swap(src, i, j):
        send(src, block(at(STEPS[i], STEPS[j])), SWAP + 4 * i + j, other)

    def first_out():
        send(w.at[0], block(me), A_IN, at(1, 0))

    def first_back():
        send(w.at[0], block(me), A_IN + 1, at(-1, 0))

    def along(i):
        src, there = w.at[0] if i == 0 else block(at(STEPS[i], 0)), block(at(STEPS[i], 0))
        send(src, there, B_IN + 3 * i, at(0, TURN[i]))

    def against(i):
        src, there = w.at[0] if i == 0 else block(at(STEPS[i], 0)), block(at(STEPS[i], 0))
        send(src, there, B_IN + 3 * i + 1, at(0, -TURN[i]))

    def first_near():
        here = block(at(-1, 0))
        arrived(here, A_IN)
        send(here, here, A_IN + 2, at(1, 0))
        swap(here, 1, 0)

    def first_behind():
        here = block(at(1, 0))
        arrived(here, A_IN + 1)
        swap(here, 2, 0)

    def first_far():
        here = block(at(2, 0))
        arrived(here, A_IN + 2)
        swap(here, 3, 0)

    def second_near(i):
        here = block(at(STEPS[i], -TURN[i]))
        arrived(here, B_IN + 3 * i)
        send(here, here, B_IN + 3 * i + 2, at(0, TURN[i]))
        swap(here, i, STEPS.index(-TURN[i]))

    def second_behind(i):
        here = block(at(STEPS[i], TURN[i]))
        arrived(here, B_IN + 3 * i + 1)
        swap(here, i, STEPS.index(TURN[i]))

    def second_far(i):
        here = block(at(STEPS[i], 2))
        arrived(here, B_IN + 3 * i + 2)
        swap(here, i, 3)

    def swapped(i, ys=STEPS):
        for step in ys:
            j = STEPS.index(step) if isinstance(step, int) else 1 + lax.div(step + 1, 2)
            x, y = mod(cx + STEPS[i], SIDE), mod(cy + step, SIDE)
            number = SWAP + (4 * j + i) * (1 - core) + (4 * i + j) * core
            arrived(block((x * SIDE + y) * 2 + 1 - core), number)

    def send_q():
        for r in range(2):
            for g in range(2):
                rows = pl.ds(CHUNK * r, CHUNK)
                send(pre.at[0, rows, pl.ds(2 * D + PIECE * g, PIECE)], piece(qraw, r, g), Q_IN + 2 * r + g, before)

    send_q()
    first_out()
    first_back()
    swap(w.at[0], 0, 0)
    along(0)
    against(0)

    def activate(group, target):
        def step(i, carry):
            rows = pl.ds(pl.multiple_of(i * 32, 32), 32)
            value = pre_v[rows, pl.ds(D * group, D)].astype(F32)
            s = sigmoid(value)
            act = value * s
            target[rows, :] = act.astype(BF16)
            slopes[rows, pl.ds(D * group, D)] = s + act * (1.0 - s)
            return carry

        local[group].wait()
        lax.fori_loop(0, TILE // 32, step, 0)

    def head_columns(h):
        return pl.ds(pl.multiple_of(h * HEAD_DIM, HEAD_DIM), HEAD_DIM)

    def weigh(scores, first_row=None):
        z = scores * SCALE
        s = sigmoid(z)
        p = z * s
        slope = s + p * (1.0 - s)
        if first_row is not None:
            row = lax.broadcasted_iota(jnp.int32, scores.shape, 0) + first_row
            keep = lax.broadcasted_iota(jnp.int32, scores.shape, 1) <= row
            p = jnp.where(keep, p, 0.0)
            slope = jnp.where(keep, slope, 0.0)
        return p.astype(BF16), slope.astype(BF16)

    def same_forward(r):
        keys = CHUNK * (r + 1)

        def step(h, carry):
            cols = head_columns(h)
            p, slope = weigh(dot_nt(qbuf[chunk(r), cols], kbuf[0:keys, cols]), CHUNK * r)
            p_same[h, chunk(r), 0:keys] = p
            s_same[h, chunk(r), 0:keys] = slope
            if keys < TILE:
                p_same[h, chunk(r), keys:TILE] = jnp.zeros((CHUNK, TILE - keys), BF16)
                s_same[h, chunk(r), keys:TILE] = jnp.zeros((CHUNK, TILE - keys), BF16)
            mix[chunk(r), cols] = dot_nn(p, vbuf[0:keys, cols]) * (1.0 / TILE)
            return carry

        lax.fori_loop(0, HEADS, step, 0, unroll=UNROLL)

    def cross_forward(r, g):
        arrived(piece(qraw, r, g), Q_IN + 2 * r + g)
        value = qraw[chunk(r), columns(g)].astype(F32)
        qx[chunk(r), columns(g)] = (value * sigmoid(value)).astype(BF16)

        def step(h, carry):
            cols = head_columns(h)
            p, slope = weigh(dot_nt(qx[chunk(r), cols], kbuf[:, cols]))
            p_cross[h, chunk(r), :] = p
            s_cross[h, chunk(r), :] = slope
            o_stage[chunk(r), cols] = (dot_nn(p, vbuf[:, cols]) * (1.0 / TILE)).astype(BF16)
            return carry

        lax.fori_loop(GROUP * g, GROUP * (g + 1), step, 0, unroll=UNROLL)
        send(piece(o_stage, r, g), piece(oraw, r, g), O_IN + 2 * r + g, after)

    def norm(r):
        for g in range(2):
            arrived(piece(oraw, r, g), O_IN + 2 * r + g)

        def step(i, carry):
            start = CHUNK * r + i * 32
            rows = pl.ds(pl.multiple_of(start, 32), 32)
            mixed = mix[rows, :] + oraw[rows, :].astype(F32) * takes
            centered = mixed - jnp.mean(mixed, axis=-1, keepdims=True)
            inv_std = lax.rsqrt(jnp.mean(centered * centered, axis=-1, keepdims=True) + EPSILON)
            normed = centered * inv_std
            live = lax.broadcasted_iota(jnp.int32, (32, 1), 0) + start < valid
            cot = jnp.where(live, og_v[rows, :].astype(F32), 0.0)
            grads[rows, pl.ds(0, D)] = (cot * normed * slopes[rows, pl.ds(0, D)]).astype(BF16)
            grad_norm = cot * gate_buf[rows, :].astype(F32)
            grad_mix = inv_std * (
                grad_norm
                - jnp.mean(grad_norm, axis=-1, keepdims=True)
                - normed * jnp.mean(grad_norm * normed, axis=-1, keepdims=True)
            )
            dobuf[rows, :] = grad_mix.astype(BF16)
            do_stage[rows, :] = (grad_mix * takes).astype(BF16)
            return carry

        lax.fori_loop(0, CHUNK // 32, step, 0, unroll=UNROLL)
        for g in range(2):
            send(piece(do_stage, r, g), piece(doraw, r, g), DO_IN + 2 * r + g, before)

    def same_backward(r):
        keys = CHUNK * (r + 1)

        def step(h, carry):
            cols = head_columns(h)
            dp = dot_nt(dobuf[chunk(r), cols], vbuf[0:keys, cols])
            ds = (dp * s_same[h, chunk(r), 0:keys].astype(F32)).astype(BF16)
            s_same[h, chunk(r), 0:keys] = ds
            dq_sum[chunk(r), cols] = dot_nn(ds, kbuf[0:keys, cols]) * (SCALE / TILE)
            return carry

        lax.fori_loop(0, HEADS, step, 0, unroll=UNROLL)

    def cross_backward(r, g):
        arrived(piece(doraw, r, g), DO_IN + 2 * r + g)

        def step(h, carry):
            cols = head_columns(h)
            dp = dot_nt(doraw[chunk(r), cols], vbuf[:, cols])
            ds = (dp * s_cross[h, chunk(r), :].astype(F32)).astype(BF16)
            s_cross[h, chunk(r), :] = ds
            dq_stage[chunk(r), cols] = (dot_nn(ds, kbuf[:, cols]) * (SCALE / TILE)).astype(BF16)
            return carry

        lax.fori_loop(GROUP * g, GROUP * (g + 1), step, 0, unroll=UNROLL)
        send(piece(dq_stage, r, g), piece(dqraw, r, g), DQ_IN + 2 * r + g, after)

    def finish_kv(g):
        def step(h, carry):
            cols = head_columns(h)
            dv = (dot_tn(p_same[h], dobuf[:, cols]) + dot_tn(p_cross[h], doraw[:, cols])) * (1.0 / TILE)
            dk = (dot_tn(s_same[h], qbuf[:, cols]) + dot_tn(s_cross[h], qx[:, cols])) * (SCALE / TILE)
            for i, value in ((1, dv), (3, dk)):
                there = pl.ds(pl.multiple_of(D * i + h * HEAD_DIM, HEAD_DIM), HEAD_DIM)
                grads[:, there] = (value * slopes[:, there]).astype(BF16)
            return carry

        lax.fori_loop(GROUP * g, GROUP * (g + 1), step, 0, unroll=UNROLL)

    def finish_q(r, g):
        arrived(piece(dqraw, r, g), DQ_IN + 2 * r + g)
        there = pl.ds(2 * D + PIECE * g, PIECE)
        dq = dq_sum[chunk(r), columns(g)] + dqraw[chunk(r), columns(g)].astype(F32)
        grads[chunk(r), there] = (dq * slopes[chunk(r), there]).astype(BF16)

    def out_copy(i, half=None, number_of=0):
        start, size = mod(cx + STEPS[i], SIDE) * TILE, TILE
        src, number = staged.at[i], OUT + i
        if half is not None:
            start, size = start + half * CHUNK, CHUNK
            src, number = staged.at[i, :, pl.ds(pl.multiple_of(half * CHUNK, CHUNK), CHUNK)], OUT + i + number_of
        cols = pl.ds(pl.multiple_of(start, CHUNK), size)
        return copy(src, out.at[0, :, cols], number, {"section": mod(section - 1, SECTIONS)})

    def project(i):
        rows = pl.ds(pl.multiple_of(mod(cx + STEPS[i], SIDE) * TILE, TILE), TILE)
        staged[i] = dot_nt(grads[...], wbuf[rows, :]).astype(BF16)

        @pl.when(section > 0)
        def _():
            out_copy(i).start()

    near_half = lax.div(cy, 2)
    beside = 1 - 2 * lax.rem(cy, 2)

    def project_half(half, number_of):
        start = mod(cx + STEPS[3], SIDE) * TILE + half * CHUNK
        rows = pl.ds(pl.multiple_of(start, CHUNK), CHUNK)
        cols = pl.ds(pl.multiple_of(half * CHUNK, CHUNK), CHUNK)
        staged[3, :, cols] = dot_nt(grads[...], wbuf[rows, :]).astype(BF16)

        @pl.when(section > 0)
        def _():
            out_copy(3, half, number_of).start()

    activate(2, qbuf)
    activate(3, kbuf)
    activate(1, vbuf)
    same_forward(0)
    first_near()
    along(1)
    against(1)
    cross_forward(0, 0)
    cross_forward(0, 1)
    first_behind()
    along(2)
    against(2)

    local[6].wait()
    local[7].wait()
    end = jnp.int32(0)
    place = jnp.int32(0)
    total = jnp.int32(0)
    for user in range(DEVICES):
        length = len_ref[0, user]
        begin = end
        end = begin + lax.div(length + (TILE - 1), TILE)
        mine = jnp.logical_and(begin <= me, me < end)
        place = jnp.where(mine, me - begin, place)
        total = jnp.where(mine, length, total)
    valid = jnp.minimum(total - place * TILE, TILE)
    linked = jnp.where(jnp.logical_and(place >= 1, link_ref[0, 0] == 1), 1, 0).astype(jnp.int32)
    takes = linked.astype(F32)

    same_forward(1)
    cross_forward(1, 0)
    cross_forward(1, 1)
    first_far()
    along(3)
    against(3)
    second_near(0)
    activate(0, gate_buf)
    local[4].wait()
    local[5].wait()
    norm(0)
    second_behind(0)
    norm(1)
    second_near(1)
    same_backward(0)
    second_behind(1)
    cross_backward(0, 0)
    cross_backward(0, 1)
    second_near(2)
    same_backward(1)
    second_behind(2)
    cross_backward(1, 0)
    cross_backward(1, 1)
    second_near(3)
    second_far(0)
    second_far(1)
    finish_kv(0)
    finish_kv(1)
    second_behind(3)
    second_far(2)
    for r in range(2):
        for g in range(2):
            finish_q(r, g)
    for i in range(3):
        swapped(i)
        project(i)
    swapped(3, (0, beside))
    project_half(near_half, 0)
    second_far(3)
    swapped(3, (-beside, 2))
    project_half(1 - near_half, 1)

    for number in sent:
        moved = piece(o_stage, 0, 0) if number >= Q_IN else block(0)
        copy(moved, moved, number, {"seq": other}).wait_send()

    @pl.when(section > 0)
    def _():
        for i in range(3):
            out_copy(i).wait_send()
        out_copy(3, near_half, 0).wait_send()
        out_copy(3, 1 - near_half, 1).wait_send()

    @pl.when(section < SECTIONS - 1)
    def _():
        for i in range(3):
            out_copy(i).wait_recv()
        out_copy(3, near_half, 0).wait_recv()
        out_copy(3, 1 - near_half, 1).wait_recv()

    @pl.when(section == SECTIONS - 1)
    def _():
        mix[...] = jnp.zeros_like(mix)
        o_stage[...] = mix[...].astype(BF16)
        zeros = pltpu.make_async_copy(o_stage, out.at[0], local_sem.at[0])
        zeros.start()
        zeros.wait()


def body(pre_act, out_grad, proj_weight, lengths, link_bits):
    wide = pltpu.VMEM((TILE, D), BF16)
    all_columns = pltpu.VMEM((TILE, 4 * D), BF16)
    totals = pltpu.VMEM((TILE, D), F32)
    scores = pltpu.VMEM((HEADS, TILE, TILE), BF16)
    hbm = pl.BlockSpec(memory_space=pltpu.HBM)
    return pl.pallas_call(
        kernel,
        out_shape=pltpu.VMEM((1, TILE, D), BF16),
        in_specs=[hbm] * 5,
        out_specs=pl.BlockSpec(memory_space=pl.ANY),
        scratch_shapes=[
            pltpu.SMEM((1, DEVICES), jnp.int32),
            pltpu.SMEM((1, 1), jnp.int32),
            all_columns,
            wide,
            pltpu.VMEM((D, 4 * D), BF16),
            wide, wide, wide, wide,
            pltpu.VMEM((TILE, 4 * D), F32),
            wide, wide, wide, wide, wide, wide, wide, wide, wide,
            scores, scores, scores, scores,
            totals, totals,
            all_columns,
            pltpu.VMEM((SIDE, TILE, TILE), BF16),
            pltpu.SemaphoreType.DMA((TRANSFERS,)),
            pltpu.SemaphoreType.DMA((TRANSFERS,)),
            pltpu.SemaphoreType.DMA((8,)),
        ],
        compiler_params=pltpu.CompilerParams(
            collective_id=0, has_side_effects=True, vmem_limit_bytes=63 * 1024 * 1024
        ),
    )(lengths, link_bits, pre_act, out_grad, proj_weight)


def solution(mesh):
    placed = (
        P("section", "seq", None),
        P("section", "seq", None),
        P("section", "seq", None),
        P("section", None),
        P("section", "seq"),
    )
    return jax.shard_map(
        body, mesh=mesh, in_specs=placed, out_specs=P("section", "seq", None), check_vma=False
    )
```
